128 devices in a mesh: grp: 32 (over x, y, core), tp: 4 (over z).
Axes of the slice: x: 4, y: 4, z: 4, core: 2. Of those that a mesh axis runs over, the one named last changes fastest.
Arguments:
- embedded: bfloat16 [32, 4, 256, 1024], P(None, 'tp', 'grp'), may hold values from -6 to 6
- start_state: bfloat16 [32, 4, 256, 1024], P(None, 'tp', 'grp'), may hold values from -6 to 6
- cotangent: bfloat16 [32, 4, 256, 1024], P(None, 'tp', 'grp'), may hold values from -6 to 6
- lengths: int32 [32], replicated, may hold values from 769 to 1024, as said below
- group_depth: int32 [32], replicated, may hold values from 0 to 1, as said below
- assignment: int32 [32], replicated, may hold values from 0 to 31, each once
- adapter_weight: bfloat16 [2048, 1024], P(None, 'tp'), may hold values from -0.125 to 0.125
- norm_gains: bfloat16 [4, 1024], P(None, 'tp'), may hold values from 0.099609375 to 1.8984375
- projections: bfloat16 [3, 1024, 1024], P(None, None, 'tp'), may hold values from -0.25 to 0.25
- output_weight: bfloat16 [1024, 1024], P('tp'), may hold values from -0.1875 to 0.1875
- gate_up_weight: bfloat16 [2, 1024, 2816], P(None, None, 'tp'), may hold values from -0.1875 to 0.1875
- down_weight: bfloat16 [2816, 1024], P('tp'), may hold values from -0.109375 to 0.109375
Outputs:
- latents: float32 [32, 4, 256, 1024], P(None, 'tp', 'grp')
- grad_embedded: float32 [32, 4, 256, 1024], P(None, 'tp', 'grp')
- grad_start: float32 [32, 4, 256, 1024], P(None, 'tp', 'grp')
- grad_adapter: float32 [2048, 1024], P(None, 'tp')
- grad_gains: float32 [4, 1024], P(None, 'tp')
- grad_projections: float32 [3, 1024, 1024], P(None, None, 'tp')
- grad_output: float32 [1024, 1024], P('tp')
- grad_gate_up: float32 [2, 1024, 2816], P(None, None, 'tp')
- grad_down: float32 [2816, 1024], P('tp')
The draws below stay inside these ranges and needn't reach their ends.
Inputs may be any that keep to these rules, and one draw needn't show every extreme that they name: `lengths`: some sequence has all 1024 tokens. `group_depth`: some depth group runs 1 iteration. `assignment`: a permutation: each depth group receives exactly one sequence.
All inputs are finite; a program needn't handle non-finite values.
Results may differ from the reference program's by a relative error of at most 0.033.
Values may be sent and summed in bfloat16 or wider, within the bound.
No kernel may reach another device: no remote copies, remote signals or barrier semaphores. Data moves between devices by JAX's collectives and lax.ppermute only.
A program may use at most 192 MiB of HBM per device.

```python
import math
import jax
import jax.numpy as jnp
from jax import lax

D = 1024
HEADS = 8
HEAD = 128
FF = 2816
SEQ_LEN = 1024
R_MAX = 1
SEQS = 32
QUARTER = 256
N_TP = 4


def draw_lengths(key, part):
    key = jax.random.fold_in(key, 11)
    first, second = jax.random.split(key)
    drawn = jax.random.randint(first, (SEQS,), 3 * SEQ_LEN // 4 + 1, SEQ_LEN + 1)
    chosen = jax.random.randint(second, (), 0, SEQS)
    return jnp.where(jnp.arange(SEQS) == chosen, SEQ_LEN, drawn).astype(jnp.int32)


def draw_group_depth(key, part):
    key = jax.random.fold_in(key, 23)
    first, second = jax.random.split(key)
    coins = jax.random.randint(first, (SEQS,), 0, 4)
    drawn = jnp.where(coins == 0, R_MAX - 1, R_MAX)
    chosen = jax.random.randint(second, (), 0, SEQS)
    return jnp.where(jnp.arange(SEQS) == chosen, R_MAX, drawn).astype(jnp.int32)


def block_scale(key, dims, pieces, least, high):
    def one(dim, shards_of):
        steps = jax.random.uniform(jax.random.fold_in(jax.random.fold_in(key, 6), dim), (shards_of,), jnp.float32, least / len(pieces), high / len(pieces))
        return jnp.repeat(jnp.exp(steps), dims[dim] // shards_of).reshape((-1,) + (1,) * (len(dims) - dim - 1))

    loudness = one(*pieces[0])
    for cut in pieces[1:]:
        loudness = loudness * one(*cut)
    return loudness


def scatter_about(key, shape, spread, bound, shards=(), kind=jnp.bfloat16):
    level = block_scale(key, shape, shards, -0.22, 0.18) if shards else 1.0
    entries = jax.random.normal(key, shape, jnp.float32) * spread * level
    return jnp.minimum(jnp.maximum(entries, -bound), bound).astype(kind)


def setup_inputs(seed: int = 0) -> dict:
    arg_keys = jax.random.split(jax.random.key(seed), 13)
    embedded = scatter_about(arg_keys[0], (SEQS, N_TP, QUARTER, D), 1.0, 6.0, ((1, 4), (2, 32)))
    start_state = scatter_about(arg_keys[1], (SEQS, N_TP, QUARTER, D), 1.0, 6.0, ((1, 4), (2, 32)))
    cotangent = scatter_about(arg_keys[2], (SEQS, N_TP, QUARTER, D), 1.0, 6.0, ((1, 4), (2, 32)))
    lengths = draw_lengths(jax.random.fold_in(arg_keys[12], 71), 0)
    group_depth = draw_group_depth(jax.random.fold_in(arg_keys[12], 71), 0)
    assignment = jax.random.permutation(arg_keys[5], SEQS).astype(jnp.int32)
    adapter_weight = scatter_about(arg_keys[6], (2 * D, D), (2 * D) ** -0.5, 0.125, ((1, 4),))
    norm_gains = jnp.clip(1.0 + 0.18 * jax.random.normal(arg_keys[7], (4, D), jnp.float32), 0.099609375, 1.8984375).astype(jnp.bfloat16)
    projections = scatter_about(arg_keys[8], (3, D, D), (D // 2) ** -0.5, 0.25, ((2, 4),))
    output_weight = scatter_about(arg_keys[9], (D, D), D ** -0.5, 0.1875, ((0, 4),))
    gate_up_weight = scatter_about(arg_keys[10], (2, D, FF), D ** -0.5, 0.1875, ((2, 4),))
    down_weight = scatter_about(arg_keys[11], (FF, D), FF ** -0.5, 0.109375, ((0, 4),))
    return {"embedded": embedded, "start_state": start_state, "cotangent": cotangent, "lengths": lengths, "group_depth": group_depth, "assignment": assignment, "adapter_weight": adapter_weight, "norm_gains": norm_gains, "projections": projections, "output_weight": output_weight, "gate_up_weight": gate_up_weight, "down_weight": down_weight}


epsilon = 1e-06
masked_value = -1e+30
rope_base = 10000.0

@jax.custom_vjp
def low(v):
    return lax.optimization_barrier(v.astype(jnp.bfloat16)).astype(jnp.float32)

@jax.custom_vjp
def low_back(v):
    return v

def low_keep(v):
    return (low(v), None)

def low_pass(kept, grad):
    return (grad,)

def back_keep(v):
    return (v, None)

def back_low(kept, grad):
    return (low(grad),)
low.defvjp(low_keep, low_pass)
low_back.defvjp(back_keep, back_low)

def matmul(left, right):
    return jnp.dot(left, right, precision=lax.Precision.HIGHEST)

def rms_norm(value, gain):
    return value * lax.rsqrt(lax.optimization_barrier(jnp.mean(value * value, axis=-1, keepdims=True)) + epsilon) * gain

def rotation(length):
    half = HEAD // 2
    freqs = rope_base ** (-jnp.arange(half, dtype=jnp.float32) * 2.0 / HEAD)
    angles = jnp.arange(length, dtype=jnp.float32)[:, None] * freqs[None, :]
    cosine = jnp.concatenate([jnp.cos(angles), jnp.cos(angles)], axis=-1)[:, None, :]
    sine = jnp.concatenate([jnp.sin(angles), jnp.sin(angles)], axis=-1)[:, None, :]
    return (cosine, sine)

def rotate(value, cosine, sine):
    half = value.shape[-1] // 2
    turned = jnp.concatenate([-value[..., half:], value[..., :half]], axis=-1)
    return value * cosine + turned * sine

def core_block(params, current, embed, length, cosine, sine):
    adapter, gains, projections, output_weight, gate_up, down = params
    joined = low(jnp.concatenate([current, embed], axis=-1))
    mixed = low_back(matmul(joined, adapter))
    normed = low(rms_norm(mixed, gains[0]))
    shape = (SEQ_LEN, HEADS, HEAD)
    queries = low(rotate(low_back(matmul(normed, projections[0])).reshape(shape), cosine, sine))
    key_rows = low(rotate(low_back(matmul(normed, projections[1])).reshape(shape), cosine, sine))
    values = low(low_back(matmul(normed, projections[2]))).reshape(shape)
    scores = jnp.einsum('qhd,khd->hqk', queries, key_rows, precision=lax.Precision.HIGHEST)
    scores = low_back(scores * (1.0 / math.sqrt(HEAD)))
    position = jnp.arange(SEQ_LEN, dtype=jnp.int32)
    allowed = (position[None, :] <= position[:, None]) & (position[None, :] < length)
    scores = jnp.where(allowed[None], scores, masked_value)
    exps = jnp.exp(scores - lax.optimization_barrier(jnp.max(scores, axis=-1, keepdims=True)))
    weights = low(exps / lax.optimization_barrier(jnp.sum(exps, axis=-1, keepdims=True)))
    context = jnp.einsum('hqk,khd->qhd', weights, values, precision=lax.Precision.HIGHEST)
    context = low(low_back(context.reshape(SEQ_LEN, D)))
    branch = low_back(matmul(context, output_weight))
    middle = mixed + rms_norm(branch, gains[1])
    hidden_in = low(rms_norm(middle, gains[2]))
    gate = low_back(matmul(hidden_in, gate_up[0]))
    up = low_back(matmul(hidden_in, gate_up[1]))
    hidden = low(gate * jax.nn.sigmoid(gate) * up)
    result = low_back(matmul(hidden, down))
    return middle + rms_norm(result, gains[3])

def sequence_forward(params, embed, current, depth, length):
    cosine, sine = rotation(SEQ_LEN)
    for step in range(R_MAX):
        output = core_block(params, current, embed, length, cosine, sine)
        current = jnp.where(step < depth, output, current)
    return current

def reference(embedded, start_state, cotangent, lengths, group_depth, assignment, adapter_weight, norm_gains, projections, output_weight, gate_up_weight, down_weight):
    params = (adapter_weight.astype(jnp.float32), norm_gains.astype(jnp.float32), projections.astype(jnp.float32), output_weight.astype(jnp.float32), gate_up_weight.astype(jnp.float32), down_weight.astype(jnp.float32))
    depths = group_depth[assignment]

    def one_sequence(totals, items):
        embed, current, cot, depth, length = items
        embed = embed.reshape(SEQ_LEN, D).astype(jnp.float32)
        current = current.reshape(SEQ_LEN, D).astype(jnp.float32)
        cot = cot.reshape(SEQ_LEN, D).astype(jnp.float32)

        def forward(weights, embed_in, start_in):
            return sequence_forward(weights, embed_in, start_in, depth, length)
        latent, pullback = jax.vjp(forward, params, embed, current)
        grad_params, grad_embed, grad_begin = pullback(cot)
        totals = jax.tree.map(lambda left, right: left + right, totals, grad_params)
        shape = (N_TP, QUARTER, D)
        return (totals, (latent.reshape(shape), grad_embed.reshape(shape), grad_begin.reshape(shape)))
    zeros = jax.tree.map(jnp.zeros_like, params)
    totals, outputs = lax.scan(one_sequence, zeros, (embedded, start_state, cotangent, depths, lengths))
    return (outputs[0], outputs[1], outputs[2], totals[0], totals[1], totals[2], totals[3], totals[4], totals[5])
```

```python
import functools
import math

import jax
import jax.numpy as jnp
import numpy as np
from jax import lax
from jax.experimental import pallas as pl
from jax.experimental.pallas import tpu as pltpu
from jax.sharding import PartitionSpec as P

HEAD = 128
TP = 4
GRP = 32
CHIPS = 16
EPSILON = 1e-06
MASKED = -1e30
ROPE_BASE = 10000.0
BF = jnp.bfloat16
F32 = jnp.float32
SAME_CORE = [[2 * i + c for i in range(CHIPS)] for c in range(2)]


def rms_factor(value):
    return lax.rsqrt(jnp.mean(value * value, axis=-1, keepdims=True) + EPSILON)


def rms_back(value, gain, grad):
    factor = rms_factor(value)
    scaled = grad * gain
    grad_value = factor * scaled - value * (factor * factor * factor) * jnp.mean(
        value * scaled, axis=-1, keepdims=True
    )
    return grad_value, jnp.sum(grad * value * factor, axis=0)


def send(value, shift):
    return lax.ppermute(value, "tp", [(i, (i + shift) % TP) for i in range(TP)])


def gather_pieces(value):
    return [value] + [send(value, k) for k in range(1, TP)]


def scatter_sum(parts):
    total = parts[0].astype(F32)
    for k in range(1, TP):
        total = total + send(parts[k], -k).astype(F32)
    return total


def to_partner(value):
    return lax.ppermute(value, "grp", [(i, i ^ 1) for i in range(GRP)])


def exchange(value):
    return lax.all_to_all(
        value, "grp", split_axis=0, concat_axis=0, tiled=True, axis_index_groups=SAME_CORE
    )


def reduce_chips(value):
    return jnp.sum(exchange(value).astype(F32), axis=0)


def gather_chips(value):
    return exchange(jnp.broadcast_to(value[None], (CHIPS,) + value.shape))


def dot(left, right):
    return jnp.dot(left, right, preferred_element_type=F32)


def dot_t(left, right):
    return lax.dot_general(left, right, (((1,), (1,)), ((), ())), preferred_element_type=F32)


def t_dot(left, right):
    return lax.dot_general(left, right, (((0,), (0,)), ((), ())), preferred_element_type=F32)


def rope_tables(length):
    half = HEAD // 2
    freqs = (ROPE_BASE ** (-np.arange(half, dtype=np.float64) * 2.0 / HEAD)).astype(np.float32)
    angles = np.arange(length, dtype=np.float32)[:, None] * freqs[None, :]
    cosine = np.concatenate([np.cos(angles), np.cos(angles)], axis=-1)
    sine = np.concatenate([-np.sin(angles), np.sin(angles)], axis=-1)
    return cosine.astype(np.float32), sine.astype(np.float32)


def attend_kernel(meta, p0, p1, p2, p3, cos, sin, ctx, qkv, probs):
    tp, length = meta[0], meta[1]
    rows = p0.shape[0]
    wide = p0.shape[1] // 3
    heads = wide // HEAD
    total = rows * TP
    for k, piece in enumerate((p0, p1, p2, p3)):
        where = pl.ds(pl.multiple_of(lax.rem(tp + (TP - k), TP) * rows, rows), rows)
        cosine, sine = cos[where, :], sin[where, :]
        for j in range(2 * heads):
            cols = slice(j * HEAD, (j + 1) * HEAD)
            value = piece[:, cols]
            turned = value * cosine + pltpu.roll(value, HEAD // 2, 1) * sine
            qkv[where, cols] = turned.astype(BF)
        qkv[where, 2 * wide :] = piece[:, 2 * wide :].astype(BF)
    scale = 1.0 / math.sqrt(HEAD)
    for i in range(TP):
        upto = (i + 1) * rows
        row = lax.broadcasted_iota(jnp.int32, (rows, upto), 0) + i * rows
        col = lax.broadcasted_iota(jnp.int32, (rows, upto), 1)
        allowed = (col <= row) & (col < length)
        for h in range(heads):
            cols = slice(h * HEAD, (h + 1) * HEAD)
            query = qkv[i * rows : upto, cols]
            keys = qkv[:upto, wide + h * HEAD : wide + (h + 1) * HEAD]
            values = qkv[:upto, 2 * wide + h * HEAD : 2 * wide + (h + 1) * HEAD]
            scores = jnp.where(allowed, dot_t(query, keys) * scale, MASKED)
            exps = jnp.exp(scores - jnp.max(scores, axis=-1, keepdims=True))
            weights = (exps / jnp.sum(exps, axis=-1, keepdims=True)).astype(BF)
            probs[h, i * rows : upto, :upto] = weights
            ctx[lax.rem(tp + (TP - i), TP), :, cols] = dot(weights, values).astype(BF)


def attend(meta, pieces, cosine, sine):
    rows, width = pieces[0].shape
    wide = width // 3
    heads = wide // HEAD
    length = rows * TP
    vmem = pl.BlockSpec(memory_space=pltpu.VMEM)
    return pl.pallas_call(
        attend_kernel,
        out_shape=(
            jax.ShapeDtypeStruct((TP, rows, wide), BF),
            jax.ShapeDtypeStruct((length, width), BF),
            jax.ShapeDtypeStruct((heads, length, length), BF),
        ),
        in_specs=[pl.BlockSpec(memory_space=pltpu.SMEM)] + [vmem] * 6,
        out_specs=(vmem, vmem, vmem),
        compiler_params=pltpu.CompilerParams(vmem_limit_bytes=48 * 2**20),
        cost_estimate=pl.CostEstimate(
            flops=3 * heads * length * length * HEAD,
            bytes_accessed=12 * 2**20,
            transcendentals=heads * length * length // 2,
        ),
        name="attend",
    )(meta, *pieces, cosine, sine)


def attend_back_kernel(meta, d0, d1, d2, d3, cos, sin, qkv, probs, out, grad_ctx, dkey, dval):
    tp = meta[0]
    rows, wide = d0.shape
    heads = wide // HEAD
    for k, piece in enumerate((d0, d1, d2, d3)):
        where = pl.ds(pl.multiple_of(lax.rem(tp + (TP - k), TP) * rows, rows), rows)
        grad_ctx[where, :] = piece[...]
    scale = 1.0 / math.sqrt(HEAD)

    def turn_back(grad, where):
        moved = grad * sin[where, :]
        return grad * cos[where, :] + pltpu.roll(moved, HEAD // 2, 1)

    for h in range(heads):
        cols = slice(h * HEAD, (h + 1) * HEAD)
        for i in range(TP):
            upto = (i + 1) * rows
            here = slice(i * rows, upto)
            query = qkv[here, cols]
            keys = qkv[:upto, wide + h * HEAD : wide + (h + 1) * HEAD]
            values = qkv[:upto, 2 * wide + h * HEAD : 2 * wide + (h + 1) * HEAD]
            grad = grad_ctx[here, cols]
            weights = probs[h, here, :upto]
            grad_weights = dot_t(grad, values)
            wide_weights = weights.astype(F32)
            inner = jnp.sum(wide_weights * grad_weights, axis=-1, keepdims=True)
            grad_scores = (wide_weights * (grad_weights - inner)).astype(BF)
            place = lax.rem(tp + (TP - i), TP)
            grad_query = dot(grad_scores, keys) * scale
            out[place, :, cols] = turn_back(grad_query, here).astype(BF)
            if i == 0:
                dkey[...] = jnp.zeros_like(dkey)
                dval[...] = jnp.zeros_like(dval)
            dkey[:upto, :] += t_dot(grad_scores, query)
            dval[:upto, :] += t_dot(weights, grad)
        for i in range(TP):
            here = slice(i * rows, (i + 1) * rows)
            place = lax.rem(tp + (TP - i), TP)
            out[place, :, wide + h * HEAD : wide + (h + 1) * HEAD] = turn_back(
                dkey[here, :] * scale, here
            ).astype(BF)
            out[place, :, 2 * wide + h * HEAD : 2 * wide + (h + 1) * HEAD] = dval[here, :].astype(BF)


def attend_back(meta, grads, cosine, sine, qkv, probs):
    rows, wide = grads[0].shape
    heads = wide // HEAD
    length = rows * TP
    vmem = pl.BlockSpec(memory_space=pltpu.VMEM)
    return pl.pallas_call(
        attend_back_kernel,
        out_shape=jax.ShapeDtypeStruct((TP, rows, 3 * wide), BF),
        in_specs=[pl.BlockSpec(memory_space=pltpu.SMEM)] + [vmem] * 8,
        out_specs=vmem,
        scratch_shapes=[
            pltpu.VMEM((length, wide), BF),
            pltpu.VMEM((length, HEAD), F32),
            pltpu.VMEM((length, HEAD), F32),
        ],
        compiler_params=pltpu.CompilerParams(vmem_limit_bytes=48 * 2**20),
        cost_estimate=pl.CostEstimate(
            flops=6 * heads * length * length * HEAD,
            bytes_accessed=10 * 2**20,
            transcendentals=0,
        ),
        name="attend_back",
    )(meta, *grads, cosine, sine, qkv, probs)


def route_kernel(assignment, state, embed, cot, out, cot_out):
    def one(s, carry):
        group = assignment[s]
        chip, side = lax.div(group, 2), lax.rem(group, 2)
        out[2 * chip, side] = state[s]
        out[2 * chip + 1, 1 - side] = embed[s]
        cot_out[group] = cot[s]
        return carry

    lax.fori_loop(0, state.shape[0], one, 0)


def route(assignment, state, embed, cot):
    groups, rows, width = state.shape
    vmem = pl.BlockSpec(memory_space=pltpu.VMEM)
    return pl.pallas_call(
        route_kernel,
        out_shape=(
            jax.ShapeDtypeStruct((groups, 2, rows, width), BF),
            jax.ShapeDtypeStruct((groups, rows, width), BF),
        ),
        in_specs=[pl.BlockSpec(memory_space=pltpu.SMEM)] + [vmem] * 3,
        out_specs=(vmem, vmem),
        compiler_params=pltpu.CompilerParams(vmem_limit_bytes=32 * 2**20),
        name="route",
    )(assignment, state, embed, cot)


def finish_kernel(assignment, depth, home, start, cot, out_latents, out_embed, out_start):
    def one(s, carry):
        group = assignment[s]
        chip, side = lax.div(group, 2), lax.rem(group, 2)
        ran = depth[group] > 0
        out_latents[s] = jnp.where(ran, home[group, 2].astype(F32), start[s].astype(F32))
        out_start[s] = jnp.where(ran, home[2 * chip, side].astype(F32), cot[s].astype(F32))
        out_embed[s] = jnp.where(ran, home[2 * chip + 1, 1 - side].astype(F32), 0.0)
        return carry

    lax.fori_loop(0, start.shape[0], one, 0)


def finish(assignment, depth, home, start, cot):
    vmem = pl.BlockSpec(memory_space=pltpu.VMEM)
    smem = pl.BlockSpec(memory_space=pltpu.SMEM)
    return pl.pallas_call(
        finish_kernel,
        out_shape=(jax.ShapeDtypeStruct(start.shape, F32),) * 3,
        in_specs=[smem, smem] + [vmem] * 3,
        out_specs=(vmem,) * 3,
        compiler_params=pltpu.CompilerParams(vmem_limit_bytes=32 * 2**20),
        name="finish",
    )(assignment, depth, home, start, cot)


def after(value, *others):
    return lax.optimization_barrier((value,) + others)[0]


def send_by_core(value, first, second):
    perm = []
    for group in range(GRP):
        shift = second if group % 2 else first
        perm += [(group * TP + i, group * TP + (i + shift) % TP) for i in range(TP)]
    return lax.ppermute(value, ("grp", "tp"), perm)


def adapt_kernel(meta, joined, p0, p1, p2, p3, mine, theirs, flat, adapter, gains):
    tp = meta[0]
    width = joined.shape[-1]
    wide = p0.shape[1]
    for k, piece in enumerate((p0, p1, p2, p3)):
        place = pl.multiple_of(lax.rem(tp + (TP - k), TP) * wide, wide)
        adapter[:, pl.ds(place, wide)] = piece[:width, :]
        gains[:, pl.ds(place, wide)] = piece[width:, :].astype(F32)[:8]
    for j, out in enumerate((mine, theirs)):
        tokens = joined[:, j].astype(F32).reshape(-1, width).astype(BF)
        flat[j] = tokens
        out[...] = dot(tokens, adapter[...]).astype(out.dtype)


def adapt(meta, joined, pieces):
    groups, _, rows, width = joined.shape
    rows = groups * rows
    vmem = pl.BlockSpec(memory_space=pltpu.VMEM)
    return pl.pallas_call(
        adapt_kernel,
        out_shape=(
            jax.ShapeDtypeStruct((rows, width), F32),
            jax.ShapeDtypeStruct((rows, width), BF),
            jax.ShapeDtypeStruct((2, rows, width), BF),
            jax.ShapeDtypeStruct((width, width), BF),
            jax.ShapeDtypeStruct((8, width), F32),
        ),
        in_specs=[pl.BlockSpec(memory_space=pltpu.SMEM)] + [vmem] * 5,
        out_specs=(vmem,) * 5,
        compiler_params=pltpu.CompilerParams(vmem_limit_bytes=40 * 2**20),
        name="adapt",
    )(meta, joined, *pieces)


def middle_kernel(
    meta, mixed, c0, c1, c2, c3, output_own, output_rest, gains, cot, gate_up, down, ffn,
    latents, grad_middle, grad_branch, g0, g1, g2, g3, keep, give, tokens, sums,
    weights, gates, ups, branch, sems,
):
    core, active = meta[2], meta[3].astype(F32)
    hidden = gate_up.shape[1]
    padded = weights.shape[2]
    copies = [
        pltpu.make_async_copy(gate_up, weights.at[0, :2, :hidden], sems.at[0]),
        pltpu.make_async_copy(down, weights.at[0, 2, :hidden], sems.at[1]),
    ]
    for k in range(1, TP):
        copies.append(pltpu.make_async_copy(ffn.at[k - 1], weights.at[k], sems.at[k + 1]))
    for copy in copies:
        copy.start()
    weights[0, :, hidden:, :] = jnp.zeros((3, padded - hidden, weights.shape[3]), BF)

    ctx = (c0, c1, c2, c3)
    total = dot(c0[...], output_own[...])
    for k in range(1, TP):
        total = total + dot(ctx[k][...], output_rest[k - 1])
    branch[...] = total
    middle = mixed[...] + total * rms_factor(total) * gains[1:2, :]
    grad_middle[...] = middle
    tokens[0] = (middle * rms_factor(middle) * gains[2:3, :]).astype(BF)

    result = jnp.zeros_like(total)
    for k in range(TP):
        if k == 0:
            copies[0].wait()
            copies[1].wait()
        else:
            copies[k + 1].wait()
        gate = dot_t(tokens[0], weights[k, 0])
        up = dot_t(tokens[0], weights[k, 1])
        gates[k] = gate
        ups[k] = up
        act = (gate * jax.nn.sigmoid(gate) * up).astype(BF)
        here = core == k // 2

        @pl.when(here)
        def _():
            keep[k % 2, 2] = act

        @pl.when(jnp.logical_not(here))
        def _():
            give[k % 2, 2] = act

        result = result + dot(act, weights[k, 2])
    middle = grad_middle[...]
    latents[...] = (middle + result * rms_factor(result) * gains[3:4, :]).astype(BF)

    grad_block = cot[...].astype(F32) * active
    grad_result, sums[2:3, :] = back(result, gains[3:4, :], grad_block)
    tokens[1] = grad_result.astype(BF)
    grad_hidden_in = jnp.zeros_like(total)
    for k in range(TP):
        grad_hidden = dot_t(tokens[1], weights[k, 2])
        gate, up = gates[k], ups[k]
        squashed = jax.nn.sigmoid(gate)
        grad_gate = (grad_hidden * up * squashed * (1.0 + gate * (1.0 - squashed))).astype(BF)
        grad_up = (grad_hidden * gate * squashed).astype(BF)
        here = core == k // 2

        @pl.when(here)
        def _():
            keep[k % 2, 0] = grad_gate
            keep[k % 2, 1] = grad_up

        @pl.when(jnp.logical_not(here))
        def _():
            give[k % 2, 0] = grad_gate
            give[k % 2, 1] = grad_up

        grad_hidden_in = grad_hidden_in + dot(grad_gate, weights[k, 0])
        grad_hidden_in = grad_hidden_in + dot(grad_up, weights[k, 1])
    grad, sums[1:2, :] = back(grad_middle[...], gains[2:3, :], grad_hidden_in)
    grad = cot[...].astype(F32) * active + grad
    grad_middle[...] = grad
    grad, sums[0:1, :] = back(branch[...], gains[1:2, :], grad)
    grad = grad.astype(BF)
    grad_branch[...] = grad
    g0[...] = dot_t(grad, output_own[...]).astype(BF)
    for k, out in ((1, g1), (2, g2), (3, g3)):
        out[...] = dot_t(grad, output_rest[k - 1]).astype(BF)
    sums[3:, :] = jnp.zeros((sums.shape[0] - 3, sums.shape[1]), F32)


def back(value, gain, grad):
    factor = rms_factor(value)
    scaled = grad * gain
    grad_value = factor * scaled - value * (factor * factor * factor) * jnp.mean(
        value * scaled, axis=-1, keepdims=True
    )
    return grad_value, jnp.sum(grad * value * factor, axis=0, keepdims=True)


def middle_part(meta, mixed, ctx, output_own, output_rest, gains, cot, gate_up, down, ffn):
    rows, width = mixed.shape
    wide = ctx[0].shape[1]
    padded = ffn.shape[2]
    vmem = pl.BlockSpec(memory_space=pltpu.VMEM)
    anywhere = pl.BlockSpec(memory_space=pl.ANY)
    acts = jax.ShapeDtypeStruct((2, 3, rows, padded), BF)
    return pl.pallas_call(
        middle_kernel,
        out_shape=(
            jax.ShapeDtypeStruct((rows, width), BF),
            jax.ShapeDtypeStruct((rows, width), F32),
            jax.ShapeDtypeStruct((rows, width), BF),
        )
        + (jax.ShapeDtypeStruct((rows, wide), BF),) * TP
        + (
            acts,
            acts,
            jax.ShapeDtypeStruct((2, rows, width), BF),
            jax.ShapeDtypeStruct((8, width), F32),
        ),
        in_specs=[pl.BlockSpec(memory_space=pltpu.SMEM)] + [vmem] * 9 + [anywhere] * 3,
        out_specs=(vmem,) * (3 + TP + 4),
        scratch_shapes=[
            pltpu.VMEM((TP, 3, padded, width), BF),
            pltpu.VMEM((TP, rows, padded), F32),
            pltpu.VMEM((TP, rows, padded), F32),
            pltpu.VMEM((rows, width), F32),
            pltpu.SemaphoreType.DMA((TP + 1,)),
        ],
        compiler_params=pltpu.CompilerParams(vmem_limit_bytes=60 * 2**20),
        cost_estimate=pl.CostEstimate(
            flops=12 * TP * rows * padded * width, bytes_accessed=30 * 2**20, transcendentals=0
        ),
        name="middle",
    )(meta, mixed, *ctx, output_own, output_rest, gains, cot, gate_up, down, ffn)


def ffn_grads_kernel(keep, other, tokens, tokens_other, out):
    total = t_dot(keep[0, 0], tokens[0]) + t_dot(other[0, 0], tokens_other[0])
    out[:, 0] = total.astype(BF).reshape(out.shape[0], out.shape[2], out.shape[3])


def ffn_gradients(keep, other, tokens, tokens_other):
    _, _, rows, padded = keep.shape
    width = tokens.shape[2]
    lines = padded // CHIPS
    acts = pl.BlockSpec((1, 1, rows, padded), lambda j: (j // 3, j % 3, 0, 0))
    token = pl.BlockSpec((1, rows, width), lambda j: ((j % 3) // 2, 0, 0))
    return pl.pallas_call(
        ffn_grads_kernel,
        grid=(6,),
        out_shape=jax.ShapeDtypeStruct((CHIPS, 6, lines, width), BF),
        in_specs=[acts, acts, token, token],
        out_specs=pl.BlockSpec((CHIPS, 1, lines, width), lambda j: (0, j, 0, 0)),
        compiler_params=pltpu.CompilerParams(vmem_limit_bytes=40 * 2**20),
        cost_estimate=pl.CostEstimate(
            flops=24 * rows * padded * width, bytes_accessed=20 * 2**20, transcendentals=0
        ),
        name="ffn_gradients",
    )(keep, other, tokens, tokens_other)


def last_kernel(meta, mine, theirs, flat, adapter, sums, parts, home):
    tp = meta[0]
    rows, width = mine.shape
    wide = parts.shape[2]
    for k in range(TP):
        where = pl.ds(pl.multiple_of(lax.rem(tp + (TP - k), TP) * wide, wide), wide)
        total = t_dot(flat[0], mine[:, where]) + t_dot(flat[1], theirs[:, where])
        parts[k, :width, :] = total.astype(BF)
        parts[k, width:, :] = jnp.concatenate(
            [sums[:, where], jnp.zeros((8, wide), F32)], axis=0
        ).astype(BF)
    for j, grad in enumerate((mine, theirs)):
        back_to = dot_t(grad[...], adapter[...]).reshape(GRP, rows // GRP, width)
        home[:, j] = back_to.astype(BF)


def last(meta, mine, theirs, flat, adapter, sums):
    rows, width = mine.shape
    vmem = pl.BlockSpec(memory_space=pltpu.VMEM)
    return pl.pallas_call(
        last_kernel,
        out_shape=(
            jax.ShapeDtypeStruct((TP, width + 16, width // TP), BF),
            jax.ShapeDtypeStruct((GRP, 2, rows // GRP, width), BF),
        ),
        in_specs=[pl.BlockSpec(memory_space=pltpu.SMEM)] + [vmem] * 5,
        out_specs=(vmem, vmem),
        compiler_params=pltpu.CompilerParams(vmem_limit_bytes=40 * 2**20),
        name="last",
    )(meta, mine, theirs, flat, adapter, sums)


def widen_kernel(core, mine, theirs, gate_up, down):
    lines, half = mine.shape[2], mine.shape[3]
    left = jnp.where(core[0] == 0, mine[0], theirs[0]).astype(F32)
    right = jnp.where(core[0] == 0, theirs[0], mine[0]).astype(F32)
    gate_up[:, :, :half] = left[:2]
    gate_up[:, :, half:] = right[:2]
    down[:, :half] = left[2]
    down[:, half:] = right[2]


def widen(core, mine, theirs, hidden):
    chips, _, lines, half = mine.shape
    steps = pl.cdiv(hidden, lines)
    part = pl.BlockSpec((1, 3, lines, half), lambda i: (i, 0, 0, 0))
    return pl.pallas_call(
        widen_kernel,
        grid=(steps,),
        out_shape=(
            jax.ShapeDtypeStruct((2, hidden, 2 * half), F32),
            jax.ShapeDtypeStruct((hidden, 2 * half), F32),
        ),
        in_specs=[pl.BlockSpec(memory_space=pltpu.SMEM), part, part],
        out_specs=(
            pl.BlockSpec((2, lines, 2 * half), lambda i: (0, i, 0)),
            pl.BlockSpec((lines, 2 * half), lambda i: (i, 0)),
        ),
        name="widen",
    )(core, mine, theirs)


def body(
    embedded,
    start_state,
    cotangent,
    lengths,
    group_depth,
    assignment,
    adapter_weight,
    norm_gains,
    projections,
    output_weight,
    gate_up_weight,
    down_weight,
):
    group = lax.axis_index("grp")
    tp = lax.axis_index("tp")
    core = lax.rem(group, 2)
    rows, width = embedded.shape[2] * GRP, embedded.shape[3]
    wide = projections.shape[2]
    hidden = down_weight.shape[0]
    share = -(-hidden // (8 * GRP)) * 8
    gate_up = gate_up_weight.transpose(0, 2, 1)

    def pick(first, second):
        return jnp.where(core == 0, first, second)

    outgoing, cot_outgoing = route(
        assignment, start_state[:, 0], embedded[:, 0], cotangent[:, 0]
    )
    joined = lax.all_to_all(outgoing, "grp", split_axis=0, concat_axis=0, tiled=True)

    half = lax.dynamic_slice_in_dim(adapter_weight, core * width, width, axis=0)
    half = jnp.concatenate([half, jnp.pad(norm_gains, ((0, 12), (0, 0)))], axis=0)
    half_pieces = gather_pieces(half)

    pad = ((0, 0), (0, share * GRP - hidden), (0, 0))
    ffn_share = jnp.concatenate(
        [
            lax.dynamic_slice_in_dim(jnp.pad(gate_up, pad), group * share, share, axis=1),
            lax.dynamic_slice_in_dim(jnp.pad(down_weight[None], pad), group * share, share, axis=1),
        ]
    )
    ffn_share = jnp.concatenate([send(ffn_share, k) for k in range(1, TP)])
    ffn = lax.all_gather(ffn_share, "grp", axis=1, tiled=True)
    ffn = ffn.reshape(TP - 1, 3, share * GRP, width)

    output_half = lax.dynamic_slice_in_dim(
        output_weight, core * (width // 2), width // 2, axis=1
    )
    output_half = after(output_half, *half_pieces[1:])
    output_half = jnp.stack([send(output_half, -k) for k in range(1, TP)])
    output_other = to_partner(output_half)
    output_rest = jnp.concatenate(
        [pick(output_half, output_other), pick(output_other, output_half)], axis=2
    )

    position = jnp.argmax(assignment == group)
    length = lengths[position]
    active = (group_depth[group] > 0).astype(jnp.int32)
    meta = jnp.stack([tp.astype(jnp.int32), length, core.astype(jnp.int32), active])
    cosine, sine = rope_tables(rows * TP)

    mixed, theirs, flat, adapter, gains = adapt(meta, joined, half_pieces)
    mixed = mixed + to_partner(theirs).astype(F32)
    normed = (mixed * rms_factor(mixed) * gains[0]).astype(BF)
    normed_pieces = gather_pieces(normed)
    grad_state = lax.all_to_all(
        after(cot_outgoing, normed), "grp", split_axis=0, concat_axis=0, tiled=True
    ).reshape(rows, width)
    merged = projections.transpose(1, 0, 2).reshape(width, 3 * wide)
    ctx, qkv, probs = attend(
        after(meta, grad_state), [dot(piece, merged) for piece in normed_pieces], cosine, sine
    )
    ctx_pieces = [ctx[0]] + [send(ctx[k], -k) for k in range(1, TP)]
    latents, grad_middle, grad_branch, g0, g1, g2, g3, keep, give, tokens, sums = middle_part(
        meta, mixed, ctx_pieces, output_weight, output_rest, gains, grad_state, gate_up,
        down_weight, ffn,
    )

    ffn_grads = ffn_gradients(keep, to_partner(give), tokens, to_partner(tokens))
    ffn_grads = lax.psum_scatter(
        ffn_grads.reshape(-1, width), "grp", scatter_dimension=0, tiled=True, axis_index_groups=SAME_CORE
    ).reshape(6, -1, width)

    grad_ctx = [g0] + [send(g, k) for k, g in ((1, g1), (2, g2), (3, g3))]
    near, far = jnp.concatenate(ctx_pieces[:2], axis=1), jnp.concatenate(ctx_pieces[2:], axis=1)
    kept, other = pick(near, far), to_partner(pick(far, near))
    grad_output = t_dot(kept, grad_branch) + t_dot(other, to_partner(grad_branch))
    grad_output = grad_output.astype(BF)

    grad_qkv = attend_back(meta, grad_ctx, cosine, sine, qkv, probs)
    grad_normed = scatter_sum([dot_t(grad_qkv[k], merged).astype(BF) for k in range(TP)])
    grad_proj = t_dot(jnp.concatenate(normed_pieces), grad_qkv.reshape(TP * rows, 3 * wide))
    grad_proj = grad_proj.astype(BF)

    top, low = grad_proj[: width // 2], grad_proj[width // 2 :]
    part = (pick(top, low).astype(F32) + to_partner(pick(low, top)).astype(F32)).astype(BF)
    lines = width // 2 // CHIPS
    part = part.reshape(CHIPS, 4, lines // 4, 3, wide).transpose(0, 3, 2, 1, 4)
    part = part.reshape(CHIPS, 3 * lines // 4, width)
    bands = wide // CHIPS
    out_part = grad_output.reshape(2, CHIPS, bands, width).transpose(1, 0, 2, 3)
    out_part = out_part.reshape(CHIPS, 2 * bands, width)
    summed = reduce_chips(jnp.concatenate([out_part, part], axis=1))
    out_part = summed[: 2 * bands].astype(BF)
    out_part = send_by_core(out_part[:bands], 0, 2).astype(F32) + send_by_core(
        out_part[bands:], 1, 3
    ).astype(F32)
    out_part = out_part + to_partner(out_part)
    out_part = lax.dynamic_slice_in_dim(out_part, core * (bands // 2), bands // 2, axis=0)
    small = jnp.concatenate([out_part, summed[2 * bands :]]).astype(BF)

    grad_mixed, gain_one = rms_back(mixed, gains[0], grad_normed)
    grad_mixed = (grad_middle + grad_mixed).astype(BF)
    sums = jnp.concatenate([gain_one[None], sums[:7]])
    parts, grad_joined = last(meta, grad_mixed, to_partner(grad_mixed), flat, adapter, sums)

    home = jnp.concatenate([grad_joined, latents.reshape(GRP, 1, 8, width)], axis=1)
    home = lax.all_to_all(home, "grp", split_axis=0, concat_axis=0, tiled=True)
    latents, grad_embedded, grad_start = finish(
        assignment, group_depth, home, start_state[:, 0], cotangent[:, 0]
    )

    total = scatter_sum([parts[k] for k in range(TP)]).astype(BF)
    lines = width // CHIPS
    gains_part = jnp.broadcast_to(total[None, width : width + 8], (CHIPS, 8, wide))
    total = jnp.concatenate([total[:width].reshape(CHIPS, lines, wide), gains_part], axis=1)
    total = reduce_chips(total)
    grad_gains = total[lines : lines + 4]
    grad_gains = grad_gains + to_partner(grad_gains)

    packed = total[:lines].astype(BF).reshape(4, lines // 4, wide).transpose(1, 0, 2)
    packed = packed.reshape(lines // 4, width)
    small = gather_chips(jnp.concatenate([small, packed]))
    small_other = to_partner(small)
    small = jnp.stack([pick(small, small_other), pick(small_other, small)], axis=1)
    at = bands // 2
    grad_output = small[:, :, :at].astype(F32).reshape(wide, width)
    lines = width // 2 // CHIPS
    to = at + 3 * lines // 4
    grad_proj = small[:, :, at:to].reshape(CHIPS, 2, 3, lines // 4, 4, wide)
    grad_proj = grad_proj.transpose(2, 1, 0, 4, 3, 5).reshape(3, width, wide).astype(F32)
    lines = width // CHIPS
    grad_adapter = small[:, :, to:].reshape(CHIPS, 2, lines // 4, 4, wide)
    grad_adapter = grad_adapter.transpose(1, 0, 3, 2, 4).reshape(2 * width, wide).astype(F32)

    part = send_by_core(ffn_grads[:3], 0, 2).astype(F32)
    part = part + send_by_core(ffn_grads[3:], -1, -3).astype(F32)
    part = part + to_partner(part.astype(BF)).astype(F32)
    part = lax.dynamic_slice_in_dim(part, core * (width // 2), width // 2, axis=2).astype(BF)
    mine = gather_chips(part)
    grad_gate_up, grad_down = widen(
        core.astype(jnp.int32).reshape(1), mine, to_partner(mine), hidden
    )

    return (
        latents[:, None],
        grad_embedded[:, None],
        grad_start[:, None],
        grad_adapter,
        grad_gains,
        grad_proj,
        grad_output,
        grad_gate_up.transpose(0, 2, 1),
        grad_down,
    )


def solution(mesh):
    tokens = P(None, "tp", "grp", None)
    weights = (
        P(None, "tp"),
        P(None, "tp"),
        P(None, None, "tp"),
        P("tp", None),
        P(None, None, "tp"),
        P("tp", None),
    )
    return jax.shard_map(
        body,
        mesh=mesh,
        in_specs=(tokens, tokens, tokens, P(), P(), P()) + weights,
        out_specs=(tokens, tokens, tokens) + weights,
        check_vma=False,
    )
```

```python
import functools
import math

import jax
import jax.numpy as jnp
import numpy as np
from jax import lax
from jax.experimental import pallas as pl
from jax.experimental.pallas import tpu as pltpu
from jax.sharding import PartitionSpec as P

HEAD = 128
TP = 4
GRP = 32
CHIPS = 16
EPSILON = 1e-06
MASKED = -1e30
ROPE_BASE = 10000.0
BF = jnp.bfloat16
F32 = jnp.float32
SAME_CORE = [[2 * i + c for i in range(CHIPS)] for c in range(2)]


def rms_factor(value):
    return lax.rsqrt(jnp.mean(value * value, axis=-1, keepdims=True) + EPSILON)


def rms_back(value, gain, grad):
    factor = rms_factor(value)
    scaled = grad * gain
    grad_value = factor * scaled - value * (factor * factor * factor) * jnp.mean(
        value * scaled, axis=-1, keepdims=True
    )
    return grad_value, jnp.sum(grad * value * factor, axis=0)


def send(value, shift):
    return lax.ppermute(value, "tp", [(i, (i + shift) % TP) for i in range(TP)])


def gather_pieces(value):
    return [value] + [send(value, k) for k in range(1, TP)]


def scatter_sum(parts):
    total = parts[0].astype(F32)
    for k in range(1, TP):
        total = total + send(parts[k], -k).astype(F32)
    return total


def gather_halves(value):
    top, low = jnp.split(value, 2, axis=0)
    up_top, down_low = send(top, 1), send(low, -1)
    up_low, down_top = send(low, 1), send(top, -1)
    far_top, far_low = send(up_top, 1), send(down_low, -1)
    return [top, low, up_top, up_low, far_top, far_low, down_top, down_low]


def scatter_halves(parts):
    own, down, far, up = [jnp.split(v, 2, axis=0) for v in parts]
    up_far, down_far = send(far[0], 1), send(far[1], -1)
    up_low, down_top = send(up[1], 1), send(down[0], -1)
    up_top = send((up[0].astype(F32) + up_far.astype(F32)).astype(BF), 1)
    down_low = send((down[1].astype(F32) + down_far.astype(F32)).astype(BF), -1)
    top = own[0].astype(F32) + down_top.astype(F32) + up_top.astype(F32)
    low = own[1].astype(F32) + up_low.astype(F32) + down_low.astype(F32)
    return jnp.concatenate([top, low])


def along(value, axis, shift):
    perm = []
    for group in range(GRP):
        x, y, core = group // 8, group // 2 % 4, group % 2
        x, y = ((x + shift) % 4, y) if axis == "x" else (x, (y + shift) % 4)
        perm.append((group, x * 8 + y * 2 + core))
    return lax.ppermute(value, "grp", perm)


def to_partner(value):
    return lax.ppermute(value, "grp", [(i, i ^ 1) for i in range(GRP)])


def exchange(value):
    return lax.all_to_all(
        value, "grp", split_axis=0, concat_axis=0, tiled=True, axis_index_groups=SAME_CORE
    )


def reduce_chips(value):
    return jnp.sum(exchange(value).astype(F32), axis=0)


def gather_chips(value):
    return exchange(jnp.broadcast_to(value[None], (CHIPS,) + value.shape))


def dot(left, right):
    return jnp.dot(left, right, preferred_element_type=F32)


def dot_t(left, right):
    return lax.dot_general(left, right, (((1,), (1,)), ((), ())), preferred_element_type=F32)


def t_dot(left, right):
    return lax.dot_general(left, right, (((0,), (0,)), ((), ())), preferred_element_type=F32)


def rope_tables(length):
    half = HEAD // 2
    freqs = (ROPE_BASE ** (-np.arange(half, dtype=np.float64) * 2.0 / HEAD)).astype(np.float32)
    angles = np.arange(length, dtype=np.float32)[:, None] * freqs[None, :]
    cosine = np.concatenate([np.cos(angles), np.cos(angles)], axis=-1)
    sine = np.concatenate([-np.sin(angles), np.sin(angles)], axis=-1)
    return cosine.astype(np.float32), sine.astype(np.float32)


def attend_kernel(meta, p0, p1, p2, p3, p4, p5, p6, p7, weights, cos, sin, ctx, qkv, probs):
    tp, length = meta[0], meta[1]
    part = p0.shape[0]
    rows = 2 * part
    wide = weights.shape[2]
    heads = wide // HEAD
    for k, piece in enumerate((p0, p1, p2, p3, p4, p5, p6, p7)):
        place = lax.rem(tp + (TP - k // 2), TP) * rows + (k % 2) * part
        where = pl.ds(pl.multiple_of(place, part), part)
        cosine, sine = cos[where, :], sin[where, :]
        for j in range(3):
            value = dot(piece[...], weights[j])
            for h in range(heads):
                head = value[:, h * HEAD : (h + 1) * HEAD]
                if j < 2:
                    head = head * cosine + pltpu.roll(head, HEAD // 2, 1) * sine
                qkv[where, j * wide + h * HEAD : j * wide + (h + 1) * HEAD] = head.astype(BF)
    scale = 1.0 / math.sqrt(HEAD)
    for i in range(TP):
        upto = (i + 1) * rows
        row = lax.broadcasted_iota(jnp.int32, (rows, upto), 0) + i * rows
        col = lax.broadcasted_iota(jnp.int32, (rows, upto), 1)
        allowed = (col <= row) & (col < length)
        for h in range(heads):
            cols = slice(h * HEAD, (h + 1) * HEAD)
            query = qkv[i * rows : upto, cols]
            keys = qkv[:upto, wide + h * HEAD : wide + (h + 1) * HEAD]
            values = qkv[:upto, 2 * wide + h * HEAD : 2 * wide + (h + 1) * HEAD]
            scores = jnp.where(allowed, dot_t(query, keys) * scale, MASKED)
            exps = jnp.exp(scores - jnp.max(scores, axis=-1, keepdims=True))
            weights_here = (exps / jnp.sum(exps, axis=-1, keepdims=True)).astype(BF)
            probs[h, i * rows : upto, :upto] = weights_here
            ctx[lax.rem(tp + (TP - i), TP), :, cols] = dot(weights_here, values).astype(BF)


def attend(meta, pieces, weights, cosine, sine):
    part, _ = pieces[0].shape
    wide = weights.shape[2]
    heads = wide // HEAD
    length = part * 2 * TP
    vmem = pl.BlockSpec(memory_space=pltpu.VMEM)
    return pl.pallas_call(
        attend_kernel,
        out_shape=(
            jax.ShapeDtypeStruct((TP, 2 * part, wide), BF),
            pltpu.HBM((length, 3 * wide), BF),
            pltpu.HBM((heads, length, length), BF),
        ),
        in_specs=[pl.BlockSpec(memory_space=pltpu.SMEM)] + [vmem] * 11,
        out_specs=(vmem, vmem, vmem),
        compiler_params=pltpu.CompilerParams(vmem_limit_bytes=20 * 2**20),
        name="attend",
    )(meta, *pieces, *in_hbm(weights, cosine, sine))


def attend_back_kernel(
    meta, d0, d1, d2, d3, cos, sin, qkv, probs, weights, out, n0, n1, n2, n3, grad_ctx, dkey, dval
):
    tp = meta[0]
    rows, wide = d0.shape
    heads = wide // HEAD
    for k, piece in enumerate((d0, d1, d2, d3)):
        where = pl.ds(pl.multiple_of(lax.rem(tp + (TP - k), TP) * rows, rows), rows)
        grad_ctx[where, :] = piece[...]
    scale = 1.0 / math.sqrt(HEAD)

    def turn_back(grad, where):
        moved = grad * sin[where, :]
        return grad * cos[where, :] + pltpu.roll(moved, HEAD // 2, 1)

    for h in range(heads):
        cols = slice(h * HEAD, (h + 1) * HEAD)
        for i in range(TP):
            upto = (i + 1) * rows
            here = slice(i * rows, upto)
            query = qkv[here, cols]
            keys = qkv[:upto, wide + h * HEAD : wide + (h + 1) * HEAD]
            values = qkv[:upto, 2 * wide + h * HEAD : 2 * wide + (h + 1) * HEAD]
            grad = grad_ctx[here, cols]
            shares = probs[h, here, :upto]
            grad_shares = dot_t(grad, values)
            wide_shares = shares.astype(F32)
            inner = jnp.sum(wide_shares * grad_shares, axis=-1, keepdims=True)
            grad_scores = (wide_shares * (grad_shares - inner)).astype(BF)
            grad_query = dot(grad_scores, keys) * scale
            out[here, cols] = turn_back(grad_query, here).astype(BF)
            if i == 0:
                dkey[...] = jnp.zeros_like(dkey)
                dval[...] = jnp.zeros_like(dval)
            dkey[:upto, :] += t_dot(grad_scores, query)
            dval[:upto, :] += t_dot(shares, grad)
        for i in range(TP):
            here = slice(i * rows, (i + 1) * rows)
            out[here, wide + h * HEAD : wide + (h + 1) * HEAD] = turn_back(
                dkey[here, :] * scale, here
            ).astype(BF)
            out[here, 2 * wide + h * HEAD : 2 * wide + (h + 1) * HEAD] = dval[here, :].astype(BF)
    for k, normed in enumerate((n0, n1, n2, n3)):
        here = pl.ds(pl.multiple_of(lax.rem(tp + (TP - k), TP) * rows, rows), rows)
        total = dot_t(out[here, :wide], weights[0])
        total = total + dot_t(out[here, wide : 2 * wide], weights[1])
        total = total + dot_t(out[here, 2 * wide :], weights[2])
        normed[...] = total.astype(BF)


def attend_back(meta, grads, cosine, sine, qkv, probs, weights):
    rows, wide = grads[0].shape
    width = weights.shape[1]
    length = rows * TP
    vmem = pl.BlockSpec(memory_space=pltpu.VMEM)
    return pl.pallas_call(
        attend_back_kernel,
        out_shape=(
            pltpu.HBM((length, 3 * wide), BF),
        )
        + (jax.ShapeDtypeStruct((rows, width), BF),) * TP,
        in_specs=[pl.BlockSpec(memory_space=pltpu.SMEM)] + [vmem] * 9,
        out_specs=(vmem,) * (1 + TP),
        scratch_shapes=[
            pltpu.VMEM((length, wide), BF),
            pltpu.VMEM((length, HEAD), F32),
            pltpu.VMEM((length, HEAD), F32),
        ],
        compiler_params=pltpu.CompilerParams(vmem_limit_bytes=22 * 2**20),
        name="attend_back",
    )(meta, *grads, *in_hbm(cosine, sine, qkv, probs, weights))


def route_kernel(assignment, state_hbm, embed_hbm, cot_hbm, out, state, embed, cot, sems):
    copies = [
        pltpu.make_async_copy(source, target, sems.at[i])
        for i, (source, target) in enumerate(((state_hbm, state), (embed_hbm, embed), (cot_hbm, cot)))
    ]
    for copy in copies:
        copy.start()
    for copy in copies:
        copy.wait()

    def one(s, carry):
        group = assignment[s]
        chip, side = lax.div(group, 2), lax.rem(group, 2)
        out[2 * chip, side] = state[s]
        out[2 * chip + 1, 1 - side] = embed[s]
        out[group, 2] = cot[s]
        return carry

    lax.fori_loop(0, state.shape[0], one, 0)


def route(assignment, state, embed, cot):
    groups, rows, width = state.shape
    vmem = pl.BlockSpec(memory_space=pltpu.VMEM)
    return pl.pallas_call(
        route_kernel,
        out_shape=jax.ShapeDtypeStruct((groups, 3, rows, width), BF),
        in_specs=[pl.BlockSpec(memory_space=pltpu.SMEM)] + [pl.BlockSpec(memory_space=pltpu.HBM)] * 3,
        out_specs=vmem,
        scratch_shapes=[pltpu.VMEM(state.shape, BF)] * 3 + [pltpu.SemaphoreType.DMA((3,))],
        compiler_params=pltpu.CompilerParams(vmem_limit_bytes=8 * 2**20),
        name="route",
    )(assignment, *in_hbm(state, embed, cot))


def finish_kernel(assignment, depth, home, start, cot, out_latents, out_embed, out_start):
    def one(s, carry):
        group = assignment[s]
        chip, side = lax.div(group, 2), lax.rem(group, 2)
        ran = depth[group] > 0
        out_latents[s] = jnp.where(ran, home[group, 2].astype(F32), start[s].astype(F32))
        out_start[s] = jnp.where(ran, home[2 * chip, side].astype(F32), cot[s].astype(F32))
        out_embed[s] = jnp.where(ran, home[2 * chip + 1, 1 - side].astype(F32), 0.0)
        return carry

    lax.fori_loop(0, start.shape[0], one, 0)


def finish(assignment, depth, home, start, cot):
    vmem = pl.BlockSpec(memory_space=pltpu.VMEM)
    smem = pl.BlockSpec(memory_space=pltpu.SMEM)
    return pl.pallas_call(
        finish_kernel,
        out_shape=(jax.ShapeDtypeStruct(start.shape, F32),) * 3,
        in_specs=[smem, smem] + [vmem] * 3,
        out_specs=(vmem,) * 3,
        compiler_params=pltpu.CompilerParams(vmem_limit_bytes=10 * 2**20),
        name="finish",
    )(assignment, depth, home, *in_hbm(start, cot))


def in_hbm(*values):
    return [pltpu.with_memory_space_constraint(v, pltpu.HBM) for v in values]


def after(value, *others):
    return lax.optimization_barrier((value,) + others)[0]


def send_by_core(value, first, second):
    perm = []
    for group in range(GRP):
        shift = second if group % 2 else first
        perm += [(group * TP + i, group * TP + (i + shift) % TP) for i in range(TP)]
    return lax.ppermute(value, ("grp", "tp"), perm)


def assemble_kernel(meta, p0, p1, p2, p3, p4, p5, p6, p7, adapter, gains):
    tp = meta[0]
    width = adapter.shape[0]
    part, wide = p0.shape
    for k, (top, low) in enumerate(((p0, p1), (p2, p3), (p4, p5), (p6, p7))):
        place = pl.multiple_of(lax.rem(tp + (TP - k), TP) * wide, wide)
        adapter[:part, pl.ds(place, wide)] = top[...]
        adapter[part:, pl.ds(place, wide)] = low[: width - part, :]
        gains[:, pl.ds(place, wide)] = low[width - part :, :].astype(F32)[:8]


def assemble(meta, pieces):
    width = pieces[0].shape[1] * TP
    vmem = pl.BlockSpec(memory_space=pltpu.VMEM)
    return pl.pallas_call(
        assemble_kernel,
        out_shape=(
            jax.ShapeDtypeStruct((width, width), BF),
            jax.ShapeDtypeStruct((8, width), F32),
        ),
        in_specs=[pl.BlockSpec(memory_space=pltpu.SMEM)] + [vmem] * 8,
        out_specs=(vmem,) * 2,
        compiler_params=pltpu.CompilerParams(vmem_limit_bytes=10 * 2**20),
        name="assemble",
    )(meta, *pieces)


def adapt_kernel(joined, adapter, mine, theirs, flat, cot):
    width = joined.shape[-1]
    for j, out in enumerate((mine, theirs)):
        tokens = joined[:, j].astype(F32).reshape(-1, width).astype(BF)
        flat[j] = tokens
        out[...] = dot(tokens, adapter[...]).astype(out.dtype)
    cot[...] = joined[:, 2].astype(F32).reshape(-1, width).astype(BF)


def adapt(joined, adapter):
    groups, _, rows, width = joined.shape
    rows = groups * rows
    vmem = pl.BlockSpec(memory_space=pltpu.VMEM)
    return pl.pallas_call(
        adapt_kernel,
        out_shape=(
            jax.ShapeDtypeStruct((rows, width), F32),
            jax.ShapeDtypeStruct((rows, width), BF),
            pltpu.HBM((2, rows, width), BF),
            pltpu.HBM((rows, width), BF),
        ),
        in_specs=[vmem] * 2,
        out_specs=(vmem,) * 4,
        compiler_params=pltpu.CompilerParams(vmem_limit_bytes=16 * 2**20),
        name="adapt",
    )(joined, adapter)


def middle_kernel(
    meta, mixed, c0, c1, c2, c3, output_own, output_mine, output_theirs, gains, cot, gate_up, down, ffn,
    latents, grad_middle, g0, g1, g2, g3, keep_out, give_out, sums,
    weights, gates, ups, branch, output_rest, keep, give, sems, out_sems,
):
    core, active = meta[2], meta[3].astype(F32)
    hidden = down.shape[0]
    padded, width = weights.shape[2], weights.shape[3]
    own_slot = 2 * core
    leaving = []

    def leave(which, cols):
        for i, (source, out) in enumerate(((keep, keep_out), (give, give_out))):
            if which in (None, i):
                sem = out_sems.at[i, sum(1 for j, _ in leaving if j == i)]
                copy = pltpu.make_async_copy(source.at[:, cols], out.at[:, cols], sem)
                copy.start()
                leaving.append((i, copy))

    def own(slot):
        return (
            pltpu.make_async_copy(gate_up, weights.at[slot, :2, :hidden], sems.at[slot]),
            pltpu.make_async_copy(down, weights.at[slot, 2, :hidden], sems.at[TP]),
        )

    def others(slot):
        source = lax.rem(slot + own_slot + TP - 1, TP)
        return pltpu.make_async_copy(ffn.at[source], weights.at[slot], sems.at[slot])

    for slot in range(TP):

        @pl.when(own_slot == slot)
        def _():
            for copy in own(slot):
                copy.start()

        @pl.when(own_slot != slot)
        def _():
            others(slot).start()

    weights[own_slot, :, hidden:, :] = jnp.zeros((3, padded - hidden, width), BF)
    half = output_mine.shape[2]
    for owner, pieces in ((core, output_mine), (1 - core, output_theirs)):
        cols = pl.ds(pl.multiple_of(owner * half, half), half)
        output_rest[:, :, cols] = pieces[...]

    at = 6 * padded
    first, second = slice(at, at + width), slice(at + width, at + 2 * width)
    at = at + 2 * width
    ctx = (c0, c1, c2, c3)
    total = dot(c0[...], output_own[...])
    for k in range(1, TP):
        total = total + dot(ctx[k][...], output_rest[k - 1])
    for k, piece in enumerate(ctx):
        wide = piece.shape[1]
        for out in (keep, give):
            out[:, at + k * wide : at + (k + 1) * wide] = piece[...]
    leave(None, slice(at, at + width))
    at = at + width
    branch[...] = total
    middle = mixed[...] + total * rms_factor(total) * gains[1:2, :]
    grad_middle[...] = middle
    tokens = (middle * rms_factor(middle) * gains[2:3, :]).astype(BF)
    keep[:, first] = tokens
    give[:, first] = tokens
    leave(None, first)

    def put(k, j, value):
        out = keep if k < 2 else give
        cols = slice(((k % 2) * 3 + j) * padded, ((k % 2) * 3 + j + 1) * padded)
        out[:, cols] = value
        leave(k // 2, cols)

    result = jnp.zeros_like(total)
    for k in range(TP):

        @pl.when(own_slot == k)
        def _():
            for copy in own(k):
                copy.wait()

        @pl.when(own_slot != k)
        def _():
            others(k).wait()

        gate = dot_t(keep[:, first], weights[k, 0])
        up = dot_t(keep[:, first], weights[k, 1])
        gates[k] = gate
        ups[k] = up
        act = (gate * jax.nn.sigmoid(gate) * up).astype(BF)
        put(k, 2, act)
        result = result + dot(act, weights[k, 2])
    middle = grad_middle[...]
    latents[...] = (middle + result * rms_factor(result) * gains[3:4, :]).astype(BF)

    grad_block = cot[...].astype(F32) * active
    grad_result, sums[2:3, :] = back(result, gains[3:4, :], grad_block)
    grad_result = grad_result.astype(BF)
    keep[:, second] = grad_result
    give[:, second] = grad_result
    leave(None, second)
    grad_hidden_in = jnp.zeros_like(total)
    for k in range(TP):
        grad_hidden = dot_t(keep[:, second], weights[k, 2])
        gate, up = gates[k], ups[k]
        squashed = jax.nn.sigmoid(gate)
        grad_gate = (grad_hidden * up * squashed * (1.0 + gate * (1.0 - squashed))).astype(BF)
        grad_up = (grad_hidden * gate * squashed).astype(BF)
        put(k, 0, grad_gate)
        put(k, 1, grad_up)
        grad_hidden_in = grad_hidden_in + dot(grad_gate, weights[k, 0])
        grad_hidden_in = grad_hidden_in + dot(grad_up, weights[k, 1])
    grad, sums[1:2, :] = back(grad_middle[...], gains[2:3, :], grad_hidden_in)
    grad = cot[...].astype(F32) * active + grad
    grad_middle[...] = grad
    grad, sums[0:1, :] = back(branch[...], gains[1:2, :], grad)
    grad = grad.astype(BF)

    @pl.when(core == 0)
    def _():
        keep[:, at:] = grad[:, :half]
        give[:, at:] = grad[:, half:]

    @pl.when(core != 0)
    def _():
        keep[:, at:] = grad[:, half:]
        give[:, at:] = grad[:, :half]

    leave(None, slice(at, at + half))
    g0[...] = dot_t(grad, output_own[...]).astype(BF)
    for k, out in ((1, g1), (2, g2), (3, g3)):
        out[...] = dot_t(grad, output_rest[k - 1]).astype(BF)
    sums[3:, :] = jnp.zeros((sums.shape[0] - 3, sums.shape[1]), F32)
    for _, copy in leaving:
        copy.wait()


def back(value, gain, grad):
    factor = rms_factor(value)
    scaled = grad * gain
    grad_value = factor * scaled - value * (factor * factor * factor) * jnp.mean(
        value * scaled, axis=-1, keepdims=True
    )
    return grad_value, jnp.sum(grad * value * factor, axis=0, keepdims=True)


def middle_part(
    meta, mixed, ctx, output_own, output_mine, output_theirs, gains, cot, gate_up, down, ffn
):
    rows, width = mixed.shape
    wide = ctx[0].shape[1]
    padded = ffn.shape[2]
    vmem = pl.BlockSpec(memory_space=pltpu.VMEM)
    anywhere = pl.BlockSpec(memory_space=pl.ANY)
    shape = (rows, 6 * padded + 3 * width + width // 2)
    acts = pltpu.HBM(shape, BF)
    hbm = pl.BlockSpec(memory_space=pltpu.HBM)
    return pl.pallas_call(
        middle_kernel,
        out_shape=(
            pltpu.HBM((rows, width), BF),
            pltpu.HBM((rows, width), F32),
        )
        + (jax.ShapeDtypeStruct((rows, wide), BF),) * TP
        + (acts, acts, jax.ShapeDtypeStruct((8, width), F32)),
        in_specs=[pl.BlockSpec(memory_space=pltpu.SMEM)] + [vmem] * 10 + [anywhere] * 3,
        out_specs=(vmem,) * (2 + TP) + (hbm, hbm, vmem),
        scratch_shapes=[
            pltpu.VMEM((TP, 3, padded, width), BF),
            pltpu.VMEM((TP, rows, padded), F32),
            pltpu.VMEM((TP, rows, padded), F32),
            pltpu.VMEM((rows, width), F32),
            pltpu.VMEM((TP - 1, wide, width), BF),
            pltpu.VMEM(shape, BF),
            pltpu.VMEM(shape, BF),
            pltpu.SemaphoreType.DMA((TP + 1,)),
            pltpu.SemaphoreType.DMA((2, 10)),
        ],
        compiler_params=pltpu.CompilerParams(vmem_limit_bytes=56 * 2**20),
        name="middle",
    )(
        meta, mixed, *ctx, output_own, output_mine, output_theirs, gains, cot, gate_up, down, ffn
    )


def gradients_kernel(
    mine, theirs, first, first_other, second, second_other, c0, c0_other, c1, c1_other, b, b_other, out, *output
):
    half = first.shape[1]

    @pl.when(pl.program_id(0) == 0)
    def _():
        for i, (ctx, other) in enumerate(((c0, c0_other), (c1, c1_other))):
            total = t_dot(ctx[...], b[...]) + t_dot(other[...], b_other[...])
            for j in range(2):
                output[2 * i + j][...] = total[j * half // 2 : (j + 1) * half // 2].astype(BF)

    for cols, tokens, others in (
        (slice(0, half), first, first_other),
        (slice(half, 2 * half), second, second_other),
    ):
        total = t_dot(mine[...], tokens[...]) + t_dot(theirs[...], others[...])
        out[:, 0, :, cols] = total.reshape(out.shape[0], out.shape[2], half).astype(BF)


def gradients(mine, theirs, padded, width):
    rows = mine.shape[0]
    half = width // 2
    first = 6 * padded // half
    acts = pl.BlockSpec((rows, padded), lambda i: (0, i))

    def token(side):
        return pl.BlockSpec((rows, half), lambda i: (0, first + 2 * (lax.rem(i, 3) // 2) + side))

    shape = (CHIPS, 6, padded // CHIPS, width)
    return pl.pallas_call(
        gradients_kernel,
        grid=(6,),
        in_specs=[acts, acts, token(0), token(0), token(1), token(1)]
        + [pl.BlockSpec((rows, half), lambda i, at=at: (0, first + at)) for at in (4, 4, 5, 5, 6, 6)],
        out_specs=(pl.BlockSpec((CHIPS, 1) + shape[2:], lambda i: (0, i, 0, 0)),)
        + (pl.BlockSpec((width // TP, half), lambda i: (0, 0)),) * TP,
        out_shape=(pltpu.HBM(shape, BF),) + (jax.ShapeDtypeStruct((width // TP, half), BF),) * TP,
        compiler_params=pltpu.CompilerParams(vmem_limit_bytes=22 * 2**20),
        name="gradients",
    )(*in_hbm(mine, theirs) * 6)


def widen_kernel(meta, mine, theirs, gate_up, down):
    core = meta[0]
    units, half = mine.shape[2], mine.shape[3]
    hidden = down.shape[0]
    for owner, part in ((core, mine), (1 - core, theirs)):
        cols = pl.ds(pl.multiple_of(owner * half, half), half)
        for i in range(pl.cdiv(hidden, units)):
            rows = min(units, hidden - i * units)
            where = slice(i * units, i * units + rows)
            gate_up[:, where, cols] = part[i, :2, :rows].astype(F32)
            down[where, cols] = part[i, 2, :rows].astype(F32)


def widen(meta, mine, theirs, hidden):
    width = 2 * mine.shape[3]
    vmem = pl.BlockSpec(memory_space=pltpu.VMEM)
    return pl.pallas_call(
        widen_kernel,
        out_shape=(
            jax.ShapeDtypeStruct((2, hidden, width), F32),
            jax.ShapeDtypeStruct((hidden, width), F32),
        ),
        in_specs=[pl.BlockSpec(memory_space=pltpu.SMEM)] + [vmem] * 2,
        out_specs=(vmem, vmem),
        compiler_params=pltpu.CompilerParams(vmem_limit_bytes=20 * 2**20),
        name="widen",
    )(meta, mine, theirs)


def proj_grads_kernel(meta, p0, p1, p2, p3, p4, p5, p6, p7, grads, keep, give, normed, total):
    tp, core = meta[0], meta[2]
    part = p0.shape[0]
    for k, piece in enumerate((p0, p1, p2, p3, p4, p5, p6, p7)):
        place = lax.rem(tp + (TP - k // 2), TP) * (2 * part) + (k % 2) * part
        normed[pl.ds(pl.multiple_of(place, part), part), :] = piece[...]
    total[...] = t_dot(normed[...], grads[...])
    half = keep.shape[0]
    keep[...] = total[pl.ds(pl.multiple_of(core * half, half), half), :].astype(BF)
    give[...] = total[pl.ds(pl.multiple_of((1 - core) * half, half), half), :].astype(BF)


def proj_gradients(meta, pieces, grads):
    length, columns = grads.shape
    width = pieces[0].shape[1]
    vmem = pl.BlockSpec(memory_space=pltpu.VMEM)
    return pl.pallas_call(
        proj_grads_kernel,
        out_shape=(jax.ShapeDtypeStruct((width // 2, columns), BF),) * 2,
        in_specs=[pl.BlockSpec(memory_space=pltpu.SMEM)] + [vmem] * 9,
        out_specs=(vmem,) * 2,
        scratch_shapes=[pltpu.VMEM((length, width), BF), pltpu.VMEM((width, columns), F32)],
        compiler_params=pltpu.CompilerParams(vmem_limit_bytes=20 * 2**20),
        name="proj_gradients",
    )(meta, *pieces, grads)


def pack_kernel(mine, theirs, out):
    chips, rows, wide = out.shape
    lines = rows // 3
    for i in range(chips):
        for m in range(3):
            where = (slice(i * lines, (i + 1) * lines), slice(m * wide, (m + 1) * wide))
            total = mine[where].astype(F32) + theirs[where].astype(F32)
            out[i, m * lines : (m + 1) * lines, :] = total.astype(BF)


def pack(mine, theirs):
    rows, columns = mine.shape
    vmem = pl.BlockSpec(memory_space=pltpu.VMEM)
    return pl.pallas_call(
        pack_kernel,
        out_shape=jax.ShapeDtypeStruct((CHIPS, 3 * rows // CHIPS, columns // 3), BF),
        in_specs=[vmem] * 2,
        out_specs=vmem,
        compiler_params=pltpu.CompilerParams(vmem_limit_bytes=8 * 2**20),
        name="pack",
    )(mine, theirs)


def unpack_kernel(meta, mine, theirs, output, proj, adapter):
    core = meta[0]
    chips, _, wide = mine.shape
    bands = wide // chips
    lines = proj.shape[1] // 2 // chips
    rows = adapter.shape[0] // 2 // chips
    for owner, part in ((core, mine), (1 - core, theirs)):
        for i in range(chips):
            for j in range(2):
                cols = pl.ds(pl.multiple_of((2 * owner + j) * wide, wide), wide)
                output[i * bands : (i + 1) * bands, cols] = part[
                    i, j * bands : (j + 1) * bands
                ].astype(F32)
            at = 2 * bands
            place = pl.ds(pl.multiple_of((owner * chips + i) * lines, lines), lines)
            for m in range(3):
                proj[m, place, :] = part[i, at + m * lines : at + (m + 1) * lines].astype(F32)
            at = at + 3 * lines
            place = pl.ds(pl.multiple_of((owner * chips + i) * rows, rows), rows)
            adapter[place, :] = part[i, at:].astype(F32)


def unpack(meta, mine, theirs, width):
    wide = mine.shape[2]
    vmem = pl.BlockSpec(memory_space=pltpu.VMEM)
    return pl.pallas_call(
        unpack_kernel,
        out_shape=(
            jax.ShapeDtypeStruct((wide, width), F32),
            jax.ShapeDtypeStruct((3, width, wide), F32),
            jax.ShapeDtypeStruct((2 * width, wide), F32),
        ),
        in_specs=[pl.BlockSpec(memory_space=pltpu.SMEM)] + [vmem] * 2,
        out_specs=(vmem,) * 3,
        compiler_params=pltpu.CompilerParams(vmem_limit_bytes=16 * 2**20),
        name="unpack",
    )(meta, mine, theirs)


def last_kernel(meta, mine, theirs, flat, adapter, sums, parts, home):
    tp = meta[0]
    rows, width = mine.shape
    wide = parts.shape[2]
    for k in range(TP):
        where = pl.ds(pl.multiple_of(lax.rem(tp + (TP - k), TP) * wide, wide), wide)
        total = t_dot(flat[0], mine[:, where]) + t_dot(flat[1], theirs[:, where])
        parts[k, :width, :] = total.astype(BF)
        parts[k, width:, :] = jnp.concatenate(
            [sums[:, where], jnp.zeros((24, wide), F32)], axis=0
        ).astype(BF)
    for j, grad in enumerate((mine, theirs)):
        back_to = dot_t(grad[...], adapter[...]).reshape(GRP, rows // GRP, width)
        home[:, j] = back_to.astype(BF)


def last(meta, mine, theirs, flat, adapter, sums):
    rows, width = mine.shape
    vmem = pl.BlockSpec(memory_space=pltpu.VMEM)
    return pl.pallas_call(
        last_kernel,
        out_shape=(
            jax.ShapeDtypeStruct((TP, width + 32, width // TP), BF),
            jax.ShapeDtypeStruct((GRP, 2, rows // GRP, width), BF),
        ),
        in_specs=[pl.BlockSpec(memory_space=pltpu.SMEM)] + [vmem] * 5,
        out_specs=(vmem, vmem),
        compiler_params=pltpu.CompilerParams(vmem_limit_bytes=16 * 2**20),
        name="last",
    )(meta, mine, theirs, flat, adapter, sums)


def body(
    embedded,
    start_state,
    cotangent,
    lengths,
    group_depth,
    assignment,
    adapter_weight,
    norm_gains,
    projections,
    output_weight,
    gate_up_weight,
    down_weight,
):
    group = lax.axis_index("grp").astype(jnp.int32)
    tp = lax.axis_index("tp").astype(jnp.int32)
    core, x, y = lax.rem(group, 2), lax.div(group, 8), lax.rem(lax.div(group, 2), 4)
    rows, width = embedded.shape[2] * GRP, embedded.shape[3]
    wide = projections.shape[2]
    hidden = down_weight.shape[0]
    share = -(-hidden // (8 * GRP)) * 8

    def pick(first, second):
        return jnp.where(core == 0, first, second)

    gate_up = gate_up_weight.transpose(0, 2, 1)
    pad = ((0, 0), (0, share * GRP - hidden), (0, 0))
    ffn = jnp.concatenate(
        [
            lax.dynamic_slice_in_dim(jnp.pad(gate_up, pad), group * share, share, axis=1),
            lax.dynamic_slice_in_dim(jnp.pad(down_weight[None], pad), group * share, share, axis=1),
        ]
    )
    ffn_pieces = gather_pieces(ffn)[1:]

    outgoing = route(assignment, start_state[:, 0], embedded[:, 0], cotangent[:, 0])
    joined = lax.all_to_all(outgoing, "grp", split_axis=0, concat_axis=0, tiled=True)

    position = jnp.argmax(assignment == group)
    length = lengths[position]
    active = (group_depth[group] > 0).astype(jnp.int32)
    meta = jnp.stack([tp, length, core, active])

    half = lax.dynamic_slice_in_dim(adapter_weight, core * width, width, axis=0)
    half = jnp.concatenate([half, jnp.pad(norm_gains, ((0, 28), (0, 0)))], axis=0)
    adapter, gains = assemble(meta, gather_halves(half))
    ffn = jnp.concatenate([after(piece, joined) for piece in ffn_pieces])
    ffn = lax.all_gather(ffn, "grp", axis=1, tiled=True).reshape(TP - 1, 3, share * GRP, width)

    cosine, sine = [jnp.asarray(v) for v in rope_tables(rows * TP)]

    mixed, theirs, flat, grad_state = adapt(joined, adapter)
    mixed = mixed + to_partner(theirs).astype(F32)
    normed = (mixed * rms_factor(mixed) * gains[0]).astype(BF)
    normed_halves = gather_halves(normed)
    output_half = lax.dynamic_slice_in_dim(
        output_weight, core * (width // 2), width // 2, axis=1
    )
    output_half = after(output_half, *normed_halves[2:])
    output_mine = [send(output_half, -k) for k in range(1, TP)]
    ctx, qkv, probs = attend(
        meta, normed_halves, projections, cosine, sine
    )
    ctx_pieces = [ctx[0]] + [send(ctx[k], -k) for k in range(1, TP)]
    output_mine = jnp.stack([after(v, ctx) for v in output_mine])
    latents, grad_middle, g0, g1, g2, g3, mine, give, sums = middle_part(
        meta, mixed, ctx_pieces, output_weight, output_mine, to_partner(output_mine), gains, grad_state,
        gate_up, down_weight, ffn,
    )

    theirs = to_partner(give)
    g1, g2, g3 = [send(g, k) for k, g in ((1, g1), (2, g2), (3, g3))]
    theirs, g1, g2, g3 = lax.optimization_barrier((theirs, g1, g2, g3))

    cuts, *output_parts = gradients(mine, theirs, share * GRP, width)
    ffn_sum = lax.psum_scatter(
        cuts.reshape(-1, width), "grp", scatter_dimension=0, tiled=True, axis_index_groups=SAME_CORE
    ).reshape(6, -1, width)

    grad_qkv, *normed_parts = attend_back(
        after(meta, cuts), [g0, g1, g2, g3], cosine, sine, qkv, probs, projections
    )
    grad_normed = scatter_halves(normed_parts)
    keep, give = proj_gradients(meta, normed_halves, grad_qkv)
    proj_part = pack(keep, to_partner(give))
    proj_sum = reduce_chips(proj_part).astype(BF)
    grad_normed = after(grad_normed, proj_part)

    grad_mixed, gain_one = rms_back(mixed, gains[0], grad_normed)
    grad_mixed = (grad_middle + grad_mixed).astype(BF)
    sums = jnp.concatenate([gain_one[None], sums[:7]])
    parts, grad_joined = last(meta, grad_mixed, to_partner(grad_mixed), flat, adapter, sums)

    home = jnp.concatenate([grad_joined, latents.reshape(GRP, 1, 8, width)], axis=1)
    home = after(home, proj_sum)
    home = lax.all_to_all(home, "grp", split_axis=0, concat_axis=0, tiled=True)

    adapter_sum = scatter_halves([parts[k] for k in range(TP)]).astype(BF)
    output_parts = [after(v, adapter_sum) for v in output_parts]
    output_sum = output_parts[0].astype(F32)
    for k in range(1, TP):
        output_sum = output_sum + send(output_parts[k], k).astype(F32)
    ffn_sum = after(ffn_sum, adapter_sum, output_sum, home)
    total = send_by_core(ffn_sum[:3], 0, 2).astype(F32)
    total = total + send_by_core(ffn_sum[3:], -1, -3).astype(F32)
    total = total + to_partner(total.astype(BF)).astype(F32)
    total = lax.dynamic_slice_in_dim(total, core * (width // 2), width // 2, axis=2).astype(BF)
    ffn_sum = lax.all_gather(total, "grp", axis=0, tiled=False, axis_index_groups=SAME_CORE)

    total = adapter_sum
    lines, bands = width // CHIPS, wide // CHIPS
    total = after(total, home)
    gains_part = jnp.broadcast_to(total[None, width : width + 8], (CHIPS, 8, wide))
    output_sum = output_sum.astype(BF).reshape(CHIPS, bands, 2, wide).transpose(0, 2, 1, 3)
    total = jnp.concatenate(
        [
            output_sum.reshape(CHIPS, 2 * bands, wide),
            total[:width].reshape(CHIPS, lines, wide),
            gains_part,
        ],
        axis=1,
    )
    total = reduce_chips(total)
    at = 2 * bands
    grad_gains = total[at + lines : at + lines + 4]
    grad_gains = grad_gains + to_partner(grad_gains)
    total = total.astype(BF)
    small = gather_chips(jnp.concatenate([total[:at], proj_sum, total[at : at + lines]]))

    here = jnp.stack([core, x, y])
    latents, grad_embedded, grad_start = finish(
        assignment, group_depth, home, start_state[:, 0], cotangent[:, 0]
    )
    grad_output, grad_proj, grad_adapter = unpack(here, small, to_partner(small), width)
    grad_gate_up, grad_down = widen(here, ffn_sum, to_partner(ffn_sum), hidden)

    return (
        latents[:, None],
        grad_embedded[:, None],
        grad_start[:, None],
        grad_adapter,
        grad_gains,
        grad_proj,
        grad_output,
        grad_gate_up.transpose(0, 2, 1),
        grad_down,
    )


def solution(mesh):
    tokens = P(None, "tp", "grp", None)
    weights = (
        P(None, "tp"),
        P(None, "tp"),
        P(None, None, "tp"),
        P("tp", None),
        P(None, None, "tp"),
        P("tp", None),
    )
    return jax.shard_map(
        body,
        mesh=mesh,
        in_specs=(tokens, tokens, tokens, P(), P(), P()) + weights,
        out_specs=(tokens, tokens, tokens) + weights,
        check_vma=False,
    )
```

```python
import functools
import math

import jax
import jax.numpy as jnp
import numpy as np
from jax import lax
from jax.experimental import pallas as pl
from jax.experimental.pallas import tpu as pltpu
from jax.sharding import PartitionSpec as P

HEAD = 128
TP = 4
GRP = 32
CHIPS = 16
EPSILON = 1e-06
MASKED = -1e30
ROPE_BASE = 10000.0
BF = jnp.bfloat16
F32 = jnp.float32
SAME_CORE = [[2 * i + c for i in range(CHIPS)] for c in range(2)]


def rms_factor(value):
    return lax.rsqrt(jnp.mean(value * value, axis=-1, keepdims=True) + EPSILON)


def rms_back(value, gain, grad):
    factor = rms_factor(value)
    scaled = grad * gain
    grad_value = factor * scaled - value * (factor * factor * factor) * jnp.mean(
        value * scaled, axis=-1, keepdims=True
    )
    return grad_value, jnp.sum(grad * value * factor, axis=0)


def send(value, shift):
    return lax.ppermute(value, "tp", [(i, (i + shift) % TP) for i in range(TP)])


def gather_pieces(value):
    return [value] + [send(value, k) for k in range(1, TP)]


def scatter_sum(parts):
    total = parts[0].astype(F32)
    for k in range(1, TP):
        total = total + send(parts[k], -k).astype(F32)
    return total


def gather_halves(value):
    top, low = jnp.split(value, 2, axis=0)
    up_top, down_low = send(top, 1), send(low, -1)
    up_low, down_top = send(low, 1), send(top, -1)
    far_top, far_low = send(up_top, 1), send(down_low, -1)
    return [top, low, up_top, up_low, far_top, far_low, down_top, down_low]


def scatter_halves(parts):
    own, down, far, up = [jnp.split(v, 2, axis=0) for v in parts]
    up_far, down_far = send(far[0], 1), send(far[1], -1)
    up_low, down_top = send(up[1], 1), send(down[0], -1)
    up_top = send((up[0].astype(F32) + up_far.astype(F32)).astype(BF), 1)
    down_low = send((down[1].astype(F32) + down_far.astype(F32)).astype(BF), -1)
    top = own[0].astype(F32) + down_top.astype(F32) + up_top.astype(F32)
    low = own[1].astype(F32) + up_low.astype(F32) + down_low.astype(F32)
    return jnp.concatenate([top, low])


def along(value, axis, shift):
    perm = []
    for group in range(GRP):
        x, y, core = group // 8, group // 2 % 4, group % 2
        x, y = ((x + shift) % 4, y) if axis == "x" else (x, (y + shift) % 4)
        perm.append((group, x * 8 + y * 2 + core))
    return lax.ppermute(value, "grp", perm)


def to_partner(value):
    return lax.ppermute(value, "grp", [(i, i ^ 1) for i in range(GRP)])


def exchange(value):
    return lax.all_to_all(
        value, "grp", split_axis=0, concat_axis=0, tiled=True, axis_index_groups=SAME_CORE
    )


def reduce_chips(value):
    return jnp.sum(exchange(value).astype(F32), axis=0)


def gather_chips(value):
    return exchange(jnp.broadcast_to(value[None], (CHIPS,) + value.shape))


def dot(left, right):
    return jnp.dot(left, right, preferred_element_type=F32)


def dot_t(left, right):
    return lax.dot_general(left, right, (((1,), (1,)), ((), ())), preferred_element_type=F32)


def t_dot(left, right):
    return lax.dot_general(left, right, (((0,), (0,)), ((), ())), preferred_element_type=F32)


def rope_tables(length):
    half = HEAD // 2
    freqs = (ROPE_BASE ** (-np.arange(half, dtype=np.float64) * 2.0 / HEAD)).astype(np.float32)
    angles = np.arange(length, dtype=np.float32)[:, None] * freqs[None, :]
    cosine = np.concatenate([np.cos(angles), np.cos(angles)], axis=-1)
    sine = np.concatenate([-np.sin(angles), np.sin(angles)], axis=-1)
    return cosine.astype(np.float32), sine.astype(np.float32)


def attend_kernel(meta, p0, p1, p2, p3, p4, p5, p6, p7, weights, cos, sin, ctx, qkv, probs):
    tp, length = meta[0], meta[1]
    part = p0.shape[0]
    rows = 2 * part
    wide = weights.shape[2]
    heads = wide // HEAD
    for k, piece in enumerate((p0, p1, p2, p3, p4, p5, p6, p7)):
        place = lax.rem(tp + (TP - k // 2), TP) * rows + (k % 2) * part
        where = pl.ds(pl.multiple_of(place, part), part)
        cosine, sine = cos[where, :], sin[where, :]
        for j in range(3):
            value = dot(piece[...], weights[j])
            for h in range(heads):
                head = value[:, h * HEAD : (h + 1) * HEAD]
                if j < 2:
                    head = head * cosine + pltpu.roll(head, HEAD // 2, 1) * sine
                qkv[where, j * wide + h * HEAD : j * wide + (h + 1) * HEAD] = head.astype(BF)
    scale = 1.0 / math.sqrt(HEAD)
    for i in range(TP):
        upto = (i + 1) * rows
        row = lax.broadcasted_iota(jnp.int32, (rows, upto), 0) + i * rows
        col = lax.broadcasted_iota(jnp.int32, (rows, upto), 1)
        allowed = (col <= row) & (col < length)
        for h in range(heads):
            cols = slice(h * HEAD, (h + 1) * HEAD)
            query = qkv[i * rows : upto, cols]
            keys = qkv[:upto, wide + h * HEAD : wide + (h + 1) * HEAD]
            values = qkv[:upto, 2 * wide + h * HEAD : 2 * wide + (h + 1) * HEAD]
            scores = jnp.where(allowed, dot_t(query, keys) * scale, MASKED)
            exps = jnp.exp(scores - jnp.max(scores, axis=-1, keepdims=True))
            weights_here = (exps / jnp.sum(exps, axis=-1, keepdims=True)).astype(BF)
            probs[h, i * rows : upto, :upto] = weights_here
            ctx[lax.rem(tp + (TP - i), TP), :, cols] = dot(weights_here, values).astype(BF)


def attend(meta, pieces, weights, cosine, sine):
    part, _ = pieces[0].shape
    wide = weights.shape[2]
    heads = wide // HEAD
    length = part * 2 * TP
    vmem = pl.BlockSpec(memory_space=pltpu.VMEM)
    return pl.pallas_call(
        attend_kernel,
        out_shape=(
            jax.ShapeDtypeStruct((TP, 2 * part, wide), BF),
            pltpu.HBM((length, 3 * wide), BF),
            pltpu.HBM((heads, length, length), BF),
        ),
        in_specs=[pl.BlockSpec(memory_space=pltpu.SMEM)] + [vmem] * 11,
        out_specs=(vmem, vmem, vmem),
        compiler_params=pltpu.CompilerParams(vmem_limit_bytes=20 * 2**20),
        name="attend",
    )(meta, *pieces, *in_hbm(weights, cosine, sine))


def attend_back_kernel(
    meta, d0, d1, d2, d3, cos, sin, qkv, probs, weights, out, n0, n1, n2, n3, grad_ctx, dkey, dval
):
    tp = meta[0]
    rows, wide = d0.shape
    heads = wide // HEAD
    for k, piece in enumerate((d0, d1, d2, d3)):
        where = pl.ds(pl.multiple_of(lax.rem(tp + (TP - k), TP) * rows, rows), rows)
        grad_ctx[where, :] = piece[...]
    scale = 1.0 / math.sqrt(HEAD)

    def turn_back(grad, where):
        moved = grad * sin[where, :]
        return grad * cos[where, :] + pltpu.roll(moved, HEAD // 2, 1)

    for h in range(heads):
        cols = slice(h * HEAD, (h + 1) * HEAD)
        for i in range(TP):
            upto = (i + 1) * rows
            here = slice(i * rows, upto)
            query = qkv[here, cols]
            keys = qkv[:upto, wide + h * HEAD : wide + (h + 1) * HEAD]
            values = qkv[:upto, 2 * wide + h * HEAD : 2 * wide + (h + 1) * HEAD]
            grad = grad_ctx[here, cols]
            shares = probs[h, here, :upto]
            grad_shares = dot_t(grad, values)
            wide_shares = shares.astype(F32)
            inner = jnp.sum(wide_shares * grad_shares, axis=-1, keepdims=True)
            grad_scores = (wide_shares * (grad_shares - inner)).astype(BF)
            grad_query = dot(grad_scores, keys) * scale
            out[here, cols] = turn_back(grad_query, here).astype(BF)
            if i == 0:
                dkey[...] = jnp.zeros_like(dkey)
                dval[...] = jnp.zeros_like(dval)
            dkey[:upto, :] += t_dot(grad_scores, query)
            dval[:upto, :] += t_dot(shares, grad)
        for i in range(TP):
            here = slice(i * rows, (i + 1) * rows)
            out[here, wide + h * HEAD : wide + (h + 1) * HEAD] = turn_back(
                dkey[here, :] * scale, here
            ).astype(BF)
            out[here, 2 * wide + h * HEAD : 2 * wide + (h + 1) * HEAD] = dval[here, :].astype(BF)
    for k, normed in enumerate((n0, n1, n2, n3)):
        here = pl.ds(pl.multiple_of(lax.rem(tp + (TP - k), TP) * rows, rows), rows)
        total = dot_t(out[here, :wide], weights[0])
        total = total + dot_t(out[here, wide : 2 * wide], weights[1])
        total = total + dot_t(out[here, 2 * wide :], weights[2])
        normed[...] = total.astype(BF)


def attend_back(meta, grads, cosine, sine, qkv, probs, weights):
    rows, wide = grads[0].shape
    width = weights.shape[1]
    length = rows * TP
    vmem = pl.BlockSpec(memory_space=pltpu.VMEM)
    return pl.pallas_call(
        attend_back_kernel,
        out_shape=(
            pltpu.HBM((length, 3 * wide), BF),
        )
        + (jax.ShapeDtypeStruct((rows, width), BF),) * TP,
        in_specs=[pl.BlockSpec(memory_space=pltpu.SMEM)] + [vmem] * 9,
        out_specs=(vmem,) * (1 + TP),
        scratch_shapes=[
            pltpu.VMEM((length, wide), BF),
            pltpu.VMEM((length, HEAD), F32),
            pltpu.VMEM((length, HEAD), F32),
        ],
        compiler_params=pltpu.CompilerParams(vmem_limit_bytes=22 * 2**20),
        name="attend_back",
    )(meta, *in_hbm(*grads, cosine, sine, qkv, probs, weights))


def route_kernel(assignment, state_hbm, embed_hbm, cot_hbm, out, state, embed, cot, sems):
    copies = [
        pltpu.make_async_copy(source, target, sems.at[i])
        for i, (source, target) in enumerate(((state_hbm, state), (embed_hbm, embed), (cot_hbm, cot)))
    ]
    for copy in copies:
        copy.start()
    for copy in copies:
        copy.wait()

    def one(s, carry):
        group = assignment[s]
        chip, side = lax.div(group, 2), lax.rem(group, 2)
        out[2 * chip, side] = state[s]
        out[2 * chip + 1, 1 - side] = embed[s]
        out[group, 2] = cot[s]
        return carry

    lax.fori_loop(0, state.shape[0], one, 0)


def route(assignment, state, embed, cot):
    groups, rows, width = state.shape
    vmem = pl.BlockSpec(memory_space=pltpu.VMEM)
    return pl.pallas_call(
        route_kernel,
        out_shape=jax.ShapeDtypeStruct((groups, 3, rows, width), BF),
        in_specs=[pl.BlockSpec(memory_space=pltpu.SMEM)] + [pl.BlockSpec(memory_space=pltpu.HBM)] * 3,
        out_specs=vmem,
        scratch_shapes=[pltpu.VMEM(state.shape, BF)] * 3 + [pltpu.SemaphoreType.DMA((3,))],
        compiler_params=pltpu.CompilerParams(vmem_limit_bytes=8 * 2**20),
        name="route",
    )(assignment, *in_hbm(state, embed, cot))


def finish_kernel(assignment, depth, home, start, cot, out_latents, out_embed, out_start):
    def one(s, carry):
        group = assignment[s]
        chip, side = lax.div(group, 2), lax.rem(group, 2)
        ran = depth[group] > 0
        out_latents[s] = jnp.where(ran, home[group, 2].astype(F32), start[s].astype(F32))
        out_start[s] = jnp.where(ran, home[2 * chip, side].astype(F32), cot[s].astype(F32))
        out_embed[s] = jnp.where(ran, home[2 * chip + 1, 1 - side].astype(F32), 0.0)
        return carry

    lax.fori_loop(0, start.shape[0], one, 0)


def finish(assignment, depth, home, start, cot):
    vmem = pl.BlockSpec(memory_space=pltpu.VMEM)
    smem = pl.BlockSpec(memory_space=pltpu.SMEM)
    return pl.pallas_call(
        finish_kernel,
        out_shape=(jax.ShapeDtypeStruct(start.shape, F32),) * 3,
        in_specs=[smem, smem] + [vmem] * 3,
        out_specs=(vmem,) * 3,
        compiler_params=pltpu.CompilerParams(vmem_limit_bytes=10 * 2**20),
        name="finish",
    )(assignment, depth, home, *in_hbm(start, cot))


def in_hbm(*values):
    return [pltpu.with_memory_space_constraint(v, pltpu.HBM) for v in values]


def after(value, *others):
    return lax.optimization_barrier((value,) + others)[0]


def send_by_core(value, first, second):
    perm = []
    for group in range(GRP):
        shift = second if group % 2 else first
        perm += [(group * TP + i, group * TP + (i + shift) % TP) for i in range(TP)]
    return lax.ppermute(value, ("grp", "tp"), perm)


def assemble_kernel(meta, p0, p1, p2, p3, p4, p5, p6, p7, adapter, gains):
    tp = meta[0]
    width = adapter.shape[0]
    part, wide = p0.shape
    for k, (top, low) in enumerate(((p0, p1), (p2, p3), (p4, p5), (p6, p7))):
        place = pl.multiple_of(lax.rem(tp + (TP - k), TP) * wide, wide)
        adapter[:part, pl.ds(place, wide)] = top[...]
        adapter[part:, pl.ds(place, wide)] = low[: width - part, :]
        gains[:, pl.ds(place, wide)] = low[width - part :, :].astype(F32)[:8]


def assemble(meta, pieces):
    width = pieces[0].shape[1] * TP
    vmem = pl.BlockSpec(memory_space=pltpu.VMEM)
    return pl.pallas_call(
        assemble_kernel,
        out_shape=(
            jax.ShapeDtypeStruct((width, width), BF),
            jax.ShapeDtypeStruct((8, width), F32),
        ),
        in_specs=[pl.BlockSpec(memory_space=pltpu.SMEM)] + [vmem] * 8,
        out_specs=(vmem,) * 2,
        compiler_params=pltpu.CompilerParams(vmem_limit_bytes=10 * 2**20),
        name="assemble",
    )(meta, *in_hbm(*pieces))


def adapt_kernel(joined, adapter, mine, theirs, flat, cot):
    width = joined.shape[-1]
    for j, out in enumerate((mine, theirs)):
        tokens = joined[:, j].astype(F32).reshape(-1, width).astype(BF)
        flat[j] = tokens
        out[...] = dot(tokens, adapter[...]).astype(out.dtype)
    cot[...] = joined[:, 2].astype(F32).reshape(-1, width).astype(BF)


def adapt(joined, adapter):
    groups, _, rows, width = joined.shape
    rows = groups * rows
    vmem = pl.BlockSpec(memory_space=pltpu.VMEM)
    return pl.pallas_call(
        adapt_kernel,
        out_shape=(
            jax.ShapeDtypeStruct((rows, width), F32),
            jax.ShapeDtypeStruct((rows, width), BF),
            pltpu.HBM((2, rows, width), BF),
            pltpu.HBM((rows, width), BF),
        ),
        in_specs=[vmem] * 2,
        out_specs=(vmem,) * 4,
        compiler_params=pltpu.CompilerParams(vmem_limit_bytes=16 * 2**20),
        name="adapt",
    )(joined, adapter)


def middle_kernel(
    meta, mixed, c0, c1, c2, c3, output_own, output_mine, output_theirs, gains, cot, gate_up, down, ffn,
    latents, grad_middle, g0, g1, g2, g3, keep_out, give_out, sums,
    weights, gates, ups, branch, output_rest, keep, give, sems, out_sems,
):
    core, active = meta[2], meta[3].astype(F32)
    hidden = down.shape[0]
    padded, width = weights.shape[2], weights.shape[3]
    own_slot = 2 * core
    leaving = []

    def leave(which, cols):
        for i, (source, out) in enumerate(((keep, keep_out), (give, give_out))):
            if which in (None, i):
                sem = out_sems.at[i, sum(1 for j, _ in leaving if j == i)]
                copy = pltpu.make_async_copy(source.at[:, cols], out.at[:, cols], sem)
                copy.start()
                leaving.append((i, copy))

    def own(slot):
        return (
            pltpu.make_async_copy(gate_up, weights.at[slot, :2, :hidden], sems.at[slot]),
            pltpu.make_async_copy(down, weights.at[slot, 2, :hidden], sems.at[TP]),
        )

    def others(slot):
        source = lax.rem(slot + own_slot + TP - 1, TP)
        return pltpu.make_async_copy(ffn.at[source], weights.at[slot], sems.at[slot])

    for slot in range(TP):

        @pl.when(own_slot == slot)
        def _():
            for copy in own(slot):
                copy.start()

        @pl.when(own_slot != slot)
        def _():
            others(slot).start()

    weights[own_slot, :, hidden:, :] = jnp.zeros((3, padded - hidden, width), BF)
    half = output_mine.shape[2]
    for owner, pieces in ((core, output_mine), (1 - core, output_theirs)):
        cols = pl.ds(pl.multiple_of(owner * half, half), half)
        output_rest[:, :, cols] = pieces[...]

    at = 6 * padded
    first, second = slice(at, at + width), slice(at + width, at + 2 * width)
    at = at + 2 * width
    ctx = (c0, c1, c2, c3)
    total = dot(c0[...], output_own[...])
    for k in range(1, TP):
        total = total + dot(ctx[k][...], output_rest[k - 1])
    for k, piece in enumerate(ctx):
        wide = piece.shape[1]
        for out in (keep, give):
            out[:, at + k * wide : at + (k + 1) * wide] = piece[...]
    leave(None, slice(at, at + width))
    at = at + width
    branch[...] = total
    middle = mixed[...] + total * rms_factor(total) * gains[1:2, :]
    grad_middle[...] = middle
    tokens = (middle * rms_factor(middle) * gains[2:3, :]).astype(BF)
    keep[:, first] = tokens
    give[:, first] = tokens
    leave(None, first)

    def put(k, j, value):
        out = keep if k < 2 else give
        cols = slice(((k % 2) * 3 + j) * padded, ((k % 2) * 3 + j + 1) * padded)
        out[:, cols] = value
        leave(k // 2, cols)

    result = jnp.zeros_like(total)
    for k in range(TP):

        @pl.when(own_slot == k)
        def _():
            for copy in own(k):
                copy.wait()

        @pl.when(own_slot != k)
        def _():
            others(k).wait()

        gate = dot_t(keep[:, first], weights[k, 0])
        up = dot_t(keep[:, first], weights[k, 1])
        gates[k] = gate
        ups[k] = up
        act = (gate * jax.nn.sigmoid(gate) * up).astype(BF)
        put(k, 2, act)
        result = result + dot(act, weights[k, 2])
    middle = grad_middle[...]
    latents[...] = (middle + result * rms_factor(result) * gains[3:4, :]).astype(BF)

    grad_block = cot[...].astype(F32) * active
    grad_result, sums[2:3, :] = back(result, gains[3:4, :], grad_block)
    grad_result = grad_result.astype(BF)
    keep[:, second] = grad_result
    give[:, second] = grad_result
    leave(None, second)
    grad_hidden_in = jnp.zeros_like(total)
    for k in range(TP):
        grad_hidden = dot_t(keep[:, second], weights[k, 2])
        gate, up = gates[k], ups[k]
        squashed = jax.nn.sigmoid(gate)
        grad_gate = (grad_hidden * up * squashed * (1.0 + gate * (1.0 - squashed))).astype(BF)
        grad_up = (grad_hidden * gate * squashed).astype(BF)
        put(k, 0, grad_gate)
        put(k, 1, grad_up)
        grad_hidden_in = grad_hidden_in + dot(grad_gate, weights[k, 0])
        grad_hidden_in = grad_hidden_in + dot(grad_up, weights[k, 1])
    grad, sums[1:2, :] = back(grad_middle[...], gains[2:3, :], grad_hidden_in)
    grad = cot[...].astype(F32) * active + grad
    grad_middle[...] = grad
    grad, sums[0:1, :] = back(branch[...], gains[1:2, :], grad)
    grad = grad.astype(BF)

    @pl.when(core == 0)
    def _():
        keep[:, at:] = grad[:, :half]
        give[:, at:] = grad[:, half:]

    @pl.when(core != 0)
    def _():
        keep[:, at:] = grad[:, half:]
        give[:, at:] = grad[:, :half]

    leave(None, slice(at, at + half))
    g0[...] = dot_t(grad, output_own[...]).astype(BF)
    for k, out in ((1, g1), (2, g2), (3, g3)):
        out[...] = dot_t(grad, output_rest[k - 1]).astype(BF)
    sums[3:, :] = jnp.zeros((sums.shape[0] - 3, sums.shape[1]), F32)
    for _, copy in leaving:
        copy.wait()


def back(value, gain, grad):
    factor = rms_factor(value)
    scaled = grad * gain
    grad_value = factor * scaled - value * (factor * factor * factor) * jnp.mean(
        value * scaled, axis=-1, keepdims=True
    )
    return grad_value, jnp.sum(grad * value * factor, axis=0, keepdims=True)


def middle_part(
    meta, mixed, ctx, output_own, output_mine, output_theirs, gains, cot, gate_up, down, ffn
):
    rows, width = mixed.shape
    wide = ctx[0].shape[1]
    padded = ffn.shape[2]
    vmem = pl.BlockSpec(memory_space=pltpu.VMEM)
    anywhere = pl.BlockSpec(memory_space=pl.ANY)
    shape = (rows, 6 * padded + 3 * width + width // 2)
    acts = pltpu.HBM(shape, BF)
    hbm = pl.BlockSpec(memory_space=pltpu.HBM)
    return pl.pallas_call(
        middle_kernel,
        out_shape=(
            pltpu.HBM((rows, width), BF),
            pltpu.HBM((rows, width), F32),
        )
        + (jax.ShapeDtypeStruct((rows, wide), BF),) * TP
        + (acts, acts, jax.ShapeDtypeStruct((8, width), F32)),
        in_specs=[pl.BlockSpec(memory_space=pltpu.SMEM)] + [vmem] * 10 + [anywhere] * 3,
        out_specs=(vmem,) * (2 + TP) + (hbm, hbm, vmem),
        scratch_shapes=[
            pltpu.VMEM((TP, 3, padded, width), BF),
            pltpu.VMEM((TP, rows, padded), F32),
            pltpu.VMEM((TP, rows, padded), F32),
            pltpu.VMEM((rows, width), F32),
            pltpu.VMEM((TP - 1, wide, width), BF),
            pltpu.VMEM(shape, BF),
            pltpu.VMEM(shape, BF),
            pltpu.SemaphoreType.DMA((TP + 1,)),
            pltpu.SemaphoreType.DMA((2, 10)),
        ],
        compiler_params=pltpu.CompilerParams(vmem_limit_bytes=56 * 2**20),
        name="middle",
    )(
        meta, mixed, *ctx, output_own, output_mine, output_theirs, gains, cot, gate_up, down, ffn
    )


def gradients_kernel(
    mine, theirs, first, first_other, second, second_other, c0, c0_other, c1, c1_other, b, b_other, out, *output
):
    half = first.shape[1]

    def both(left, right):
        return jnp.concatenate([left[...], right[...]], axis=0)

    @pl.when(pl.program_id(0) == 0)
    def _():
        for i, (ctx, other) in enumerate(((c0, c0_other), (c1, c1_other))):
            total = t_dot(both(ctx, other), both(b, b_other))
            for j in range(2):
                output[2 * i + j][...] = total[j * half // 2 : (j + 1) * half // 2].astype(BF)

    tokens = jnp.concatenate([both(first, first_other), both(second, second_other)], axis=1)
    total = t_dot(both(mine, theirs), tokens)
    rows, cols = out.shape[2], out.shape[3]
    for i in range(4):
        for j in range(4):
            piece = total[i * rows : (i + 1) * rows, j * cols : (j + 1) * cols]
            out[4 * i + j, 0] = piece.astype(BF)


def gradients(mine, theirs, hidden, padded, width):
    rows = mine.shape[0]
    half = width // 2
    first = 6 * padded // half
    acts = pl.BlockSpec((rows, padded), lambda i: (0, i))

    def token(side):
        return pl.BlockSpec((rows, half), lambda i: (0, first + 2 * (lax.rem(i, 3) // 2) + side))

    shape = (CHIPS, 6, hidden // 4, width // 4)
    return pl.pallas_call(
        gradients_kernel,
        grid=(6,),
        in_specs=[acts, acts, token(0), token(0), token(1), token(1)]
        + [pl.BlockSpec((rows, half), lambda i, at=at: (0, first + at)) for at in (4, 4, 5, 5, 6, 6)],
        out_specs=(pl.BlockSpec((CHIPS, 1) + shape[2:], lambda i: (0, i, 0, 0)),)
        + (pl.BlockSpec((width // TP, half), lambda i: (0, 0)),) * TP,
        out_shape=(pltpu.HBM(shape, BF),) + (pltpu.HBM((width // TP, half), BF),) * TP,
        compiler_params=pltpu.CompilerParams(vmem_limit_bytes=22 * 2**20),
        name="gradients",
    )(*[*in_hbm(mine), theirs] * 6)


def widen_kernel(meta, mine, theirs, gate_up, down):
    core = meta[0]
    units, part = mine.shape[2], mine.shape[3]
    for owner, shares in ((core, mine), (1 - core, theirs)):
        for i in range(4):
            for j in range(4):
                rows = slice(i * units, (i + 1) * units)
                cols = pl.ds(pl.multiple_of((2 * j + owner) * part, part), part)
                gate_up[:, rows, cols] = shares[4 * i + j, :2].astype(F32)
                down[rows, cols] = shares[4 * i + j, 2].astype(F32)


def widen(meta, mine, theirs, hidden):
    width = 8 * mine.shape[3]
    vmem = pl.BlockSpec(memory_space=pltpu.VMEM)
    return pl.pallas_call(
        widen_kernel,
        out_shape=(
            jax.ShapeDtypeStruct((2, hidden, width), F32),
            jax.ShapeDtypeStruct((hidden, width), F32),
        ),
        in_specs=[pl.BlockSpec(memory_space=pltpu.SMEM)] + [vmem] * 2,
        out_specs=(vmem, vmem),
        compiler_params=pltpu.CompilerParams(vmem_limit_bytes=20 * 2**20),
        name="widen",
    )(meta, mine, theirs)


def proj_grads_kernel(meta, p0, p1, p2, p3, p4, p5, p6, p7, grads, keep, give, normed, total):
    tp, core = meta[0], meta[2]
    part = p0.shape[0]
    for k, piece in enumerate((p0, p1, p2, p3, p4, p5, p6, p7)):
        place = lax.rem(tp + (TP - k // 2), TP) * (2 * part) + (k % 2) * part
        normed[pl.ds(pl.multiple_of(place, part), part), :] = piece[...]
    total[...] = t_dot(normed[...], grads[...])
    half = keep.shape[0]
    keep[...] = total[pl.ds(pl.multiple_of(core * half, half), half), :].astype(BF)
    give[...] = total[pl.ds(pl.multiple_of((1 - core) * half, half), half), :].astype(BF)


def proj_gradients(meta, pieces, grads):
    length, columns = grads.shape
    width = pieces[0].shape[1]
    vmem = pl.BlockSpec(memory_space=pltpu.VMEM)
    return pl.pallas_call(
        proj_grads_kernel,
        out_shape=(jax.ShapeDtypeStruct((width // 2, columns), BF),) * 2,
        in_specs=[pl.BlockSpec(memory_space=pltpu.SMEM)] + [vmem] * 9,
        out_specs=(vmem,) * 2,
        scratch_shapes=[pltpu.VMEM((length, width), BF), pltpu.VMEM((width, columns), F32)],
        compiler_params=pltpu.CompilerParams(vmem_limit_bytes=20 * 2**20),
        name="proj_gradients",
    )(meta, *pieces, grads)


def pack_kernel(mine, theirs, o0, o1, o2, o3, out):
    chips, _, wide = out.shape
    lines = mine.shape[0] // chips
    bands = o0.shape[0] // chips
    total = o0[...].astype(F32) + o1[...].astype(F32) + o2[...].astype(F32) + o3[...].astype(F32)
    total = total.astype(BF)
    for i in range(chips):
        for h in range(2):
            where = (slice(i * bands, (i + 1) * bands), slice(h * wide, (h + 1) * wide))
            out[i, h * bands : (h + 1) * bands, :] = total[where]
        at = 2 * bands
        for m in range(3):
            where = (slice(i * lines, (i + 1) * lines), slice(m * wide, (m + 1) * wide))
            part = mine[where].astype(F32) + theirs[where].astype(F32)
            out[i, at + m * lines : at + (m + 1) * lines, :] = part.astype(BF)


def pack(mine, theirs, output_parts):
    rows, columns = mine.shape
    wide = columns // 3
    vmem = pl.BlockSpec(memory_space=pltpu.VMEM)
    return pl.pallas_call(
        pack_kernel,
        out_shape=jax.ShapeDtypeStruct((CHIPS, (3 * rows + 2 * wide) // CHIPS, wide), BF),
        in_specs=[vmem] * 6,
        out_specs=vmem,
        compiler_params=pltpu.CompilerParams(vmem_limit_bytes=10 * 2**20),
        name="pack",
    )(mine, theirs, *in_hbm(*output_parts))


def unpack_kernel(meta, mine, theirs, output, proj, adapter):
    core = meta[0]
    chips, _, wide = mine.shape
    bands = wide // chips
    lines = proj.shape[1] // 2 // chips
    rows = adapter.shape[0] // 2 // chips
    for owner, part in ((core, mine), (1 - core, theirs)):
        for i in range(chips):
            for j in range(2):
                cols = pl.ds(pl.multiple_of((2 * owner + j) * wide, wide), wide)
                output[i * bands : (i + 1) * bands, cols] = part[
                    i, j * bands : (j + 1) * bands
                ].astype(F32)
            at = 2 * bands
            place = pl.ds(pl.multiple_of((owner * chips + i) * lines, lines), lines)
            for m in range(3):
                proj[m, place, :] = part[i, at + m * lines : at + (m + 1) * lines].astype(F32)
            at = at + 3 * lines
            place = pl.ds(pl.multiple_of((owner * chips + i) * rows, rows), rows)
            adapter[place, :] = part[i, at:].astype(F32)


def unpack(meta, mine, theirs, width):
    wide = mine.shape[2]
    vmem = pl.BlockSpec(memory_space=pltpu.VMEM)
    return pl.pallas_call(
        unpack_kernel,
        out_shape=(
            jax.ShapeDtypeStruct((wide, width), F32),
            jax.ShapeDtypeStruct((3, width, wide), F32),
            jax.ShapeDtypeStruct((2 * width, wide), F32),
        ),
        in_specs=[pl.BlockSpec(memory_space=pltpu.SMEM)] + [vmem] * 2,
        out_specs=(vmem,) * 3,
        compiler_params=pltpu.CompilerParams(vmem_limit_bytes=16 * 2**20),
        name="unpack",
    )(meta, mine, theirs)


def last_kernel(meta, mine, theirs, flat, adapter, sums, parts, home):
    tp = meta[0]
    rows, width = mine.shape
    wide = parts.shape[2]
    for k in range(TP):
        where = pl.ds(pl.multiple_of(lax.rem(tp + (TP - k), TP) * wide, wide), wide)
        total = t_dot(flat[0], mine[:, where]) + t_dot(flat[1], theirs[:, where])
        parts[k, :width, :] = total.astype(BF)
        parts[k, width:, :] = jnp.concatenate(
            [sums[:, where], jnp.zeros((24, wide), F32)], axis=0
        ).astype(BF)
    for j, grad in enumerate((mine, theirs)):
        back_to = dot_t(grad[...], adapter[...]).reshape(GRP, rows // GRP, width)
        home[:, j] = back_to.astype(BF)


def last(meta, mine, theirs, flat, adapter, sums):
    rows, width = mine.shape
    vmem = pl.BlockSpec(memory_space=pltpu.VMEM)
    return pl.pallas_call(
        last_kernel,
        out_shape=(
            jax.ShapeDtypeStruct((TP, width + 32, width // TP), BF),
            jax.ShapeDtypeStruct((GRP, 2, rows // GRP, width), BF),
        ),
        in_specs=[pl.BlockSpec(memory_space=pltpu.SMEM)] + [vmem] * 5,
        out_specs=(vmem, vmem),
        compiler_params=pltpu.CompilerParams(vmem_limit_bytes=16 * 2**20),
        name="last",
    )(meta, mine, theirs, flat, adapter, sums)


def body(
    embedded,
    start_state,
    cotangent,
    lengths,
    group_depth,
    assignment,
    adapter_weight,
    norm_gains,
    projections,
    output_weight,
    gate_up_weight,
    down_weight,
):
    group = lax.axis_index("grp").astype(jnp.int32)
    tp = lax.axis_index("tp").astype(jnp.int32)
    core, x, y = lax.rem(group, 2), lax.div(group, 8), lax.rem(lax.div(group, 2), 4)
    rows, width = embedded.shape[2] * GRP, embedded.shape[3]
    wide = projections.shape[2]
    hidden = down_weight.shape[0]
    share = -(-hidden // (8 * GRP)) * 8

    def pick(first, second):
        return jnp.where(core == 0, first, second)

    gate_up = gate_up_weight.transpose(0, 2, 1)
    pad = ((0, 0), (0, share * GRP - hidden), (0, 0))
    ffn = jnp.concatenate(
        [
            lax.dynamic_slice_in_dim(jnp.pad(gate_up, pad), group * share, share, axis=1),
            lax.dynamic_slice_in_dim(jnp.pad(down_weight[None], pad), group * share, share, axis=1),
        ]
    )

    outgoing = route(assignment, start_state[:, 0], embedded[:, 0], cotangent[:, 0])
    joined = lax.all_to_all(outgoing, "grp", split_axis=0, concat_axis=0, tiled=True)

    position = jnp.argmax(assignment == group)
    length = lengths[position]
    active = (group_depth[group] > 0).astype(jnp.int32)
    meta = jnp.stack([tp, length, core, active])

    half = lax.dynamic_slice_in_dim(adapter_weight, core * width, width, axis=0)
    half = jnp.concatenate([half, jnp.pad(norm_gains, ((0, 28), (0, 0)))], axis=0)
    half_pieces = gather_halves(half)
    adapter, gains = assemble(meta, half_pieces)
    ffn_pieces = gather_pieces(after(ffn, *half_pieces[2:4], *half_pieces[6:]))[1:]
    ffn = jnp.concatenate([after(piece, joined) for piece in ffn_pieces])
    ffn = lax.all_gather(ffn, "grp", axis=1, tiled=True).reshape(TP - 1, 3, share * GRP, width)

    cosine, sine = [jnp.asarray(v) for v in rope_tables(rows * TP)]

    mixed, theirs, flat, grad_state = adapt(joined, adapter)
    mixed = mixed + to_partner(theirs).astype(F32)
    normed = (mixed * rms_factor(mixed) * gains[0]).astype(BF)
    normed_halves = gather_halves(normed)
    output_half = lax.dynamic_slice_in_dim(
        output_weight, core * (width // 2), width // 2, axis=1
    )
    output_half = after(output_half, *normed_halves[2:])
    output_mine = [send(output_half, -k) for k in range(1, TP)]
    ctx, qkv, probs = attend(
        meta, normed_halves, projections, cosine, sine
    )
    ctx_pieces = [ctx[0]] + [send(ctx[k], -k) for k in range(1, TP)]
    output_mine = jnp.stack([after(v, ctx) for v in output_mine])
    latents, grad_middle, g0, g1, g2, g3, mine, give, sums = middle_part(
        meta, mixed, ctx_pieces, output_weight, output_mine, to_partner(output_mine), gains, grad_state,
        gate_up, down_weight, ffn,
    )

    theirs = to_partner(give)
    g1, g2, g3 = [send(g, k) for k, g in ((1, g1), (2, g2), (3, g3))]
    theirs, g1, g2, g3 = lax.optimization_barrier((theirs, g1, g2, g3))

    cuts, *output_parts = gradients(mine, theirs, hidden, share * GRP, width)
    ffn_sum = lax.psum_scatter(
        cuts.reshape(-1, width // 4), "grp", scatter_dimension=0, tiled=True, axis_index_groups=SAME_CORE
    ).reshape(6, -1, width // 4)

    grad_qkv, *normed_parts = attend_back(
        after(meta, cuts), [g0, g1, g2, g3], cosine, sine, qkv, probs, projections
    )
    output_parts = output_parts[:1] + [send(output_parts[k], k) for k in range(1, TP)]
    grad_normed = scatter_halves([after(v, *output_parts[1:]) for v in normed_parts])
    keep, give = proj_gradients(meta, normed_halves, grad_qkv)
    some_part = pack(keep, to_partner(give), output_parts)
    grad_normed = after(grad_normed, some_part)

    grad_mixed, gain_one = rms_back(mixed, gains[0], grad_normed)
    grad_mixed = (grad_middle + grad_mixed).astype(BF)
    sums = jnp.concatenate([gain_one[None], sums[:7]])
    parts, grad_joined = last(meta, grad_mixed, to_partner(grad_mixed), flat, adapter, sums)

    adapter_sum = scatter_halves([parts[k] for k in range(TP)]).astype(BF)
    ffn_sum = after(ffn_sum, adapter_sum)
    total = send_by_core(ffn_sum[:3], 0, 2).astype(F32)
    total = total + send_by_core(ffn_sum[3:], -1, -3).astype(F32)
    total = total + to_partner(total.astype(BF)).astype(F32)
    total = lax.dynamic_slice_in_dim(total, core * (width // 8), width // 8, axis=2).astype(BF)
    ffn_part = total

    total = adapter_sum
    lines = width // CHIPS
    gains_part = jnp.broadcast_to(total[None, width : width + 8], (CHIPS, 8, wide))
    total = jnp.concatenate(
        [some_part, total[:width].reshape(CHIPS, lines, wide), gains_part], axis=1
    )
    total = reduce_chips(total)
    at = total.shape[0] - 8
    grad_gains = total[at : at + 4]
    grad_gains = grad_gains + to_partner(grad_gains)
    small = total[:at].astype(BF)
    ffn_sum = gather_chips(after(ffn_part, small))
    small = lax.all_gather(small, "grp", axis=0, tiled=False, axis_index_groups=SAME_CORE)

    home = jnp.concatenate([grad_joined, latents.reshape(GRP, 1, 8, width)], axis=1)
    home = after(home, ffn_sum)
    home = lax.all_to_all(home, "grp", split_axis=0, concat_axis=0, tiled=True)

    here = jnp.stack([core, x, y])
    grad_output, grad_proj, grad_adapter = unpack(here, small, to_partner(small), width)
    grad_gate_up, grad_down = widen(here, ffn_sum, to_partner(ffn_sum), hidden)

    home = after(home, grad_down, grad_output)
    latents, grad_embedded, grad_start = finish(
        assignment, group_depth, home, start_state[:, 0], cotangent[:, 0]
    )

    return (
        latents[:, None],
        grad_embedded[:, None],
        grad_start[:, None],
        grad_adapter,
        grad_gains,
        grad_proj,
        grad_output,
        grad_gate_up.transpose(0, 2, 1),
        grad_down,
    )


def solution(mesh):
    tokens = P(None, "tp", "grp", None)
    weights = (
        P(None, "tp"),
        P(None, "tp"),
        P(None, None, "tp"),
        P("tp", None),
        P(None, None, "tp"),
        P("tp", None),
    )
    return jax.shard_map(
        body,
        mesh=mesh,
        in_specs=(tokens, tokens, tokens, P(), P(), P()) + weights,
        out_specs=(tokens, tokens, tokens) + weights,
        check_vma=False,
    )
```

```python
import functools
import math

import jax
import jax.numpy as jnp
import numpy as np
from jax import lax
from jax.experimental import pallas as pl
from jax.experimental.pallas import tpu as pltpu
from jax.sharding import PartitionSpec as P

HEAD = 128
TP = 4
GRP = 32
CHIPS = 16
EPSILON = 1e-06
MASKED = -1e30
ROPE_BASE = 10000.0
BF = jnp.bfloat16
F32 = jnp.float32
SAME_CORE = [[2 * i + c for i in range(CHIPS)] for c in range(2)]


def rms_factor(value):
    return lax.rsqrt(jnp.mean(value * value, axis=-1, keepdims=True) + EPSILON)


def rms_back(value, gain, grad):
    factor = rms_factor(value)
    scaled = grad * gain
    grad_value = factor * scaled - value * (factor * factor * factor) * jnp.mean(
        value * scaled, axis=-1, keepdims=True
    )
    return grad_value, jnp.sum(grad * value * factor, axis=0)


def send(value, shift):
    return lax.ppermute(value, "tp", [(i, (i + shift) % TP) for i in range(TP)])


def gather_pieces(value):
    return [value] + [send(value, k) for k in range(1, TP)]


def scatter_sum(parts):
    total = parts[0].astype(F32)
    for k in range(1, TP):
        total = total + send(parts[k], -k).astype(F32)
    return total


def gather_halves(value):
    top, low = jnp.split(value, 2, axis=0)
    up_top, down_low = send(top, 1), send(low, -1)
    up_low, down_top = send(low, 1), send(top, -1)
    far_top, far_low = send(up_top, 1), send(down_low, -1)
    return [top, low, up_top, up_low, far_top, far_low, down_top, down_low]


def scatter_halves(parts):
    own, down, far, up = [jnp.split(v, 2, axis=0) for v in parts]
    up_far, down_far = send(far[0], 1), send(far[1], -1)
    up_low, down_top = send(up[1], 1), send(down[0], -1)
    up_top = send((up[0].astype(F32) + up_far.astype(F32)).astype(BF), 1)
    down_low = send((down[1].astype(F32) + down_far.astype(F32)).astype(BF), -1)
    top = own[0].astype(F32) + down_top.astype(F32) + up_top.astype(F32)
    low = own[1].astype(F32) + up_low.astype(F32) + down_low.astype(F32)
    return jnp.concatenate([top, low])


def along(value, axis, shift):
    perm = []
    for group in range(GRP):
        x, y, core = group // 8, group // 2 % 4, group % 2
        x, y = ((x + shift) % 4, y) if axis == "x" else (x, (y + shift) % 4)
        perm.append((group, x * 8 + y * 2 + core))
    return lax.ppermute(value, "grp", perm)


def to_partner(value):
    return lax.ppermute(value, "grp", [(i, i ^ 1) for i in range(GRP)])


def exchange(value):
    return lax.all_to_all(
        value, "grp", split_axis=0, concat_axis=0, tiled=True, axis_index_groups=SAME_CORE
    )


def reduce_chips(value):
    return jnp.sum(exchange(value).astype(F32), axis=0)


def gather_chips(value):
    return exchange(jnp.broadcast_to(value[None], (CHIPS,) + value.shape))


def dot(left, right):
    return jnp.dot(left, right, preferred_element_type=F32)


def dot_t(left, right):
    return lax.dot_general(left, right, (((1,), (1,)), ((), ())), preferred_element_type=F32)


def t_dot(left, right):
    return lax.dot_general(left, right, (((0,), (0,)), ((), ())), preferred_element_type=F32)


def rope_tables(length):
    half = HEAD // 2
    freqs = (ROPE_BASE ** (-np.arange(half, dtype=np.float64) * 2.0 / HEAD)).astype(np.float32)
    angles = np.arange(length, dtype=np.float32)[:, None] * freqs[None, :]
    cosine = np.concatenate([np.cos(angles), np.cos(angles)], axis=-1)
    sine = np.concatenate([-np.sin(angles), np.sin(angles)], axis=-1)
    return cosine.astype(np.float32), sine.astype(np.float32)


def attend_kernel(meta, p0, p1, p2, p3, p4, p5, p6, p7, weights, cos, sin, ctx, qkv, probs):
    tp, length = meta[0], meta[1]
    part = p0.shape[0]
    rows = 2 * part
    wide = weights.shape[2]
    heads = wide // HEAD
    for k, piece in enumerate((p0, p1, p2, p3, p4, p5, p6, p7)):
        place = lax.rem(tp + (TP - k // 2), TP) * rows + (k % 2) * part
        where = pl.ds(pl.multiple_of(place, part), part)
        cosine, sine = cos[where, :], sin[where, :]
        for j in range(3):
            value = dot(piece[...], weights[j])
            for h in range(heads):
                head = value[:, h * HEAD : (h + 1) * HEAD]
                if j < 2:
                    head = head * cosine + pltpu.roll(head, HEAD // 2, 1) * sine
                qkv[where, j * wide + h * HEAD : j * wide + (h + 1) * HEAD] = head.astype(BF)
    scale = 1.0 / math.sqrt(HEAD)
    for i in range(TP):
        upto = (i + 1) * rows
        row = lax.broadcasted_iota(jnp.int32, (rows, upto), 0) + i * rows
        col = lax.broadcasted_iota(jnp.int32, (rows, upto), 1)
        allowed = (col <= row) & (col < length)
        for h in range(heads):
            cols = slice(h * HEAD, (h + 1) * HEAD)
            query = qkv[i * rows : upto, cols]
            keys = qkv[:upto, wide + h * HEAD : wide + (h + 1) * HEAD]
            values = qkv[:upto, 2 * wide + h * HEAD : 2 * wide + (h + 1) * HEAD]
            scores = jnp.where(allowed, dot_t(query, keys) * scale, MASKED)
            exps = jnp.exp(scores - jnp.max(scores, axis=-1, keepdims=True))
            weights_here = (exps / jnp.sum(exps, axis=-1, keepdims=True)).astype(BF)
            probs[h, i * rows : upto, :upto] = weights_here
            ctx[lax.rem(tp + (TP - i), TP), :, cols] = dot(weights_here, values).astype(BF)


def attend(meta, pieces, weights, cosine, sine):
    part, _ = pieces[0].shape
    wide = weights.shape[2]
    heads = wide // HEAD
    length = part * 2 * TP
    vmem = pl.BlockSpec(memory_space=pltpu.VMEM)
    return pl.pallas_call(
        attend_kernel,
        out_shape=(
            jax.ShapeDtypeStruct((TP, 2 * part, wide), BF),
            pltpu.HBM((length, 3 * wide), BF),
            pltpu.HBM((heads, length, length), BF),
        ),
        in_specs=[pl.BlockSpec(memory_space=pltpu.SMEM)] + [vmem] * 11,
        out_specs=(vmem, vmem, vmem),
        compiler_params=pltpu.CompilerParams(vmem_limit_bytes=20 * 2**20),
        name="attend",
    )(meta, *pieces, *in_hbm(weights, cosine, sine))


def attend_back_kernel(
    meta, d0, d1, d2, d3, cos, sin, qkv, probs, weights, out, n0, n1, n2, n3, grad_ctx, dkey, dval
):
    tp = meta[0]
    rows, wide = d0.shape
    heads = wide // HEAD
    for k, piece in enumerate((d0, d1, d2, d3)):
        where = pl.ds(pl.multiple_of(lax.rem(tp + (TP - k), TP) * rows, rows), rows)
        grad_ctx[where, :] = piece[...]
    scale = 1.0 / math.sqrt(HEAD)

    def turn_back(grad, where):
        moved = grad * sin[where, :]
        return grad * cos[where, :] + pltpu.roll(moved, HEAD // 2, 1)

    for h in range(heads):
        cols = slice(h * HEAD, (h + 1) * HEAD)
        for i in range(TP):
            upto = (i + 1) * rows
            here = slice(i * rows, upto)
            query = qkv[here, cols]
            keys = qkv[:upto, wide + h * HEAD : wide + (h + 1) * HEAD]
            values = qkv[:upto, 2 * wide + h * HEAD : 2 * wide + (h + 1) * HEAD]
            grad = grad_ctx[here, cols]
            shares = probs[h, here, :upto]
            grad_shares = dot_t(grad, values)
            wide_shares = shares.astype(F32)
            inner = jnp.sum(wide_shares * grad_shares, axis=-1, keepdims=True)
            grad_scores = (wide_shares * (grad_shares - inner)).astype(BF)
            grad_query = dot(grad_scores, keys) * scale
            out[here, cols] = turn_back(grad_query, here).astype(BF)
            if i == 0:
                dkey[...] = jnp.zeros_like(dkey)
                dval[...] = jnp.zeros_like(dval)
            dkey[:upto, :] += t_dot(grad_scores, query)
            dval[:upto, :] += t_dot(shares, grad)
        for i in range(TP):
            here = slice(i * rows, (i + 1) * rows)
            out[here, wide + h * HEAD : wide + (h + 1) * HEAD] = turn_back(
                dkey[here, :] * scale, here
            ).astype(BF)
            out[here, 2 * wide + h * HEAD : 2 * wide + (h + 1) * HEAD] = dval[here, :].astype(BF)
    for k, normed in enumerate((n0, n1, n2, n3)):
        here = pl.ds(pl.multiple_of(lax.rem(tp + (TP - k), TP) * rows, rows), rows)
        total = dot_t(out[here, :wide], weights[0])
        total = total + dot_t(out[here, wide : 2 * wide], weights[1])
        total = total + dot_t(out[here, 2 * wide :], weights[2])
        normed[...] = total.astype(BF)


def attend_back(meta, grads, cosine, sine, qkv, probs, weights):
    rows, wide = grads[0].shape
    width = weights.shape[1]
    length = rows * TP
    vmem = pl.BlockSpec(memory_space=pltpu.VMEM)
    return pl.pallas_call(
        attend_back_kernel,
        out_shape=(
            pltpu.HBM((length, 3 * wide), BF),
        )
        + (jax.ShapeDtypeStruct((rows, width), BF),) * TP,
        in_specs=[pl.BlockSpec(memory_space=pltpu.SMEM)] + [vmem] * 9,
        out_specs=(vmem,) * (1 + TP),
        scratch_shapes=[
            pltpu.VMEM((length, wide), BF),
            pltpu.VMEM((length, HEAD), F32),
            pltpu.VMEM((length, HEAD), F32),
        ],
        compiler_params=pltpu.CompilerParams(vmem_limit_bytes=22 * 2**20),
        name="attend_back",
    )(meta, *in_hbm(*grads, cosine, sine, qkv, probs, weights))


def route_kernel(assignment, state_hbm, embed_hbm, cot_hbm, out, state, embed, cot, sems):
    copies = [
        pltpu.make_async_copy(source, target, sems.at[i])
        for i, (source, target) in enumerate(((state_hbm, state), (embed_hbm, embed), (cot_hbm, cot)))
    ]
    for copy in copies:
        copy.start()
    for copy in copies:
        copy.wait()

    def one(s, carry):
        group = assignment[s]
        chip, side = lax.div(group, 2), lax.rem(group, 2)
        out[2 * chip, side] = state[s]
        out[2 * chip + 1, 1 - side] = embed[s]
        out[group, 2] = cot[s]
        return carry

    lax.fori_loop(0, state.shape[0], one, 0)


def route(assignment, state, embed, cot):
    groups, rows, width = state.shape
    vmem = pl.BlockSpec(memory_space=pltpu.VMEM)
    return pl.pallas_call(
        route_kernel,
        out_shape=jax.ShapeDtypeStruct((groups, 3, rows, width), BF),
        in_specs=[pl.BlockSpec(memory_space=pltpu.SMEM)] + [pl.BlockSpec(memory_space=pltpu.HBM)] * 3,
        out_specs=vmem,
        scratch_shapes=[pltpu.VMEM(state.shape, BF)] * 3 + [pltpu.SemaphoreType.DMA((3,))],
        compiler_params=pltpu.CompilerParams(vmem_limit_bytes=8 * 2**20),
        name="route",
    )(assignment, *in_hbm(state, embed, cot))


def finish_kernel(assignment, depth, home, start, cot, out_latents, out_embed, out_start):
    def one(s, carry):
        group = assignment[s]
        chip, side = lax.div(group, 2), lax.rem(group, 2)
        ran = depth[group] > 0
        out_latents[s] = jnp.where(ran, home[group, 2].astype(F32), start[s].astype(F32))
        out_start[s] = jnp.where(ran, home[2 * chip, side].astype(F32), cot[s].astype(F32))
        out_embed[s] = jnp.where(ran, home[2 * chip + 1, 1 - side].astype(F32), 0.0)
        return carry

    lax.fori_loop(0, start.shape[0], one, 0)


def finish(assignment, depth, home, start, cot):
    vmem = pl.BlockSpec(memory_space=pltpu.VMEM)
    smem = pl.BlockSpec(memory_space=pltpu.SMEM)
    return pl.pallas_call(
        finish_kernel,
        out_shape=(jax.ShapeDtypeStruct(start.shape, F32),) * 3,
        in_specs=[smem, smem] + [vmem] * 3,
        out_specs=(vmem,) * 3,
        compiler_params=pltpu.CompilerParams(vmem_limit_bytes=10 * 2**20),
        name="finish",
    )(assignment, depth, home, *in_hbm(start, cot))


def in_hbm(*values):
    return [pltpu.with_memory_space_constraint(v, pltpu.HBM) for v in values]


def after(value, *others):
    return lax.optimization_barrier((value,) + others)[0]


def send_by_core(value, first, second):
    perm = []
    for group in range(GRP):
        shift = second if group % 2 else first
        perm += [(group * TP + i, group * TP + (i + shift) % TP) for i in range(TP)]
    return lax.ppermute(value, ("grp", "tp"), perm)


def assemble_kernel(meta, p0, p1, p2, p3, p4, p5, p6, p7, adapter, gains):
    tp = meta[0]
    width = adapter.shape[0]
    part, wide = p0.shape
    for k, (top, low) in enumerate(((p0, p1), (p2, p3), (p4, p5), (p6, p7))):
        place = pl.multiple_of(lax.rem(tp + (TP - k), TP) * wide, wide)
        adapter[:part, pl.ds(place, wide)] = top[...]
        adapter[part:, pl.ds(place, wide)] = low[: width - part, :]
        gains[:, pl.ds(place, wide)] = low[width - part :, :].astype(F32)[:8]


def assemble(meta, pieces):
    width = pieces[0].shape[1] * TP
    vmem = pl.BlockSpec(memory_space=pltpu.VMEM)
    return pl.pallas_call(
        assemble_kernel,
        out_shape=(
            jax.ShapeDtypeStruct((width, width), BF),
            jax.ShapeDtypeStruct((8, width), F32),
        ),
        in_specs=[pl.BlockSpec(memory_space=pltpu.SMEM)] + [vmem] * 8,
        out_specs=(vmem,) * 2,
        compiler_params=pltpu.CompilerParams(vmem_limit_bytes=10 * 2**20),
        name="assemble",
    )(meta, *in_hbm(*pieces))


def adapt_kernel(joined, adapter, mine, theirs, flat, cot):
    width = joined.shape[-1]
    for j, out in enumerate((mine, theirs)):
        tokens = joined[:, j].astype(F32).reshape(-1, width).astype(BF)
        flat[j] = tokens
        out[...] = dot(tokens, adapter[...]).astype(out.dtype)
    cot[...] = joined[:, 2].astype(F32).reshape(-1, width).astype(BF)


def adapt(joined, adapter):
    groups, _, rows, width = joined.shape
    rows = groups * rows
    vmem = pl.BlockSpec(memory_space=pltpu.VMEM)
    return pl.pallas_call(
        adapt_kernel,
        out_shape=(
            jax.ShapeDtypeStruct((rows, width), F32),
            jax.ShapeDtypeStruct((rows, width), BF),
            pltpu.HBM((2, rows, width), BF),
            pltpu.HBM((rows, width), BF),
        ),
        in_specs=[vmem] * 2,
        out_specs=(vmem,) * 4,
        compiler_params=pltpu.CompilerParams(vmem_limit_bytes=16 * 2**20),
        name="adapt",
    )(joined, adapter)


def middle_kernel(
    meta, mixed, c0, c1, c2, c3, output_own, output_mine, output_theirs, gains, cot, gate_up, down, ffn,
    latents, grad_middle, g0, g1, g2, g3, keep_out, give_out, sums,
    weights, gates, ups, branch, output_rest, keep, give, sems, out_sems,
):
    core, active = meta[2], meta[3].astype(F32)
    hidden = down.shape[0]
    padded, width = weights.shape[2], weights.shape[3]
    own_slot = 2 * core
    leaving = []

    def leave(which, cols):
        for i, (source, out) in enumerate(((keep, keep_out), (give, give_out))):
            if which in (None, i):
                sem = out_sems.at[i, sum(1 for j, _ in leaving if j == i)]
                copy = pltpu.make_async_copy(source.at[:, cols], out.at[:, cols], sem)
                copy.start()
                leaving.append((i, copy))

    def own(slot):
        return (
            pltpu.make_async_copy(gate_up, weights.at[slot, :2, :hidden], sems.at[slot]),
            pltpu.make_async_copy(down, weights.at[slot, 2, :hidden], sems.at[TP]),
        )

    def others(slot):
        source = lax.rem(slot + own_slot + TP - 1, TP)
        return pltpu.make_async_copy(ffn.at[source], weights.at[slot], sems.at[slot])

    for slot in range(TP):

        @pl.when(own_slot == slot)
        def _():
            for copy in own(slot):
                copy.start()

        @pl.when(own_slot != slot)
        def _():
            others(slot).start()

    weights[own_slot, :, hidden:, :] = jnp.zeros((3, padded - hidden, width), BF)
    half = output_mine.shape[2]
    for owner, pieces in ((core, output_mine), (1 - core, output_theirs)):
        cols = pl.ds(pl.multiple_of(owner * half, half), half)
        output_rest[:, :, cols] = pieces[...]

    at = 6 * padded
    first, second = slice(at, at + width), slice(at + width, at + 2 * width)
    at = at + 2 * width
    ctx = (c0, c1, c2, c3)
    total = dot(c0[...], output_own[...])
    for k in range(1, TP):
        total = total + dot(ctx[k][...], output_rest[k - 1])
    for k, piece in enumerate(ctx):
        wide = piece.shape[1]
        for out in (keep, give):
            out[:, at + k * wide : at + (k + 1) * wide] = piece[...]
    leave(None, slice(at, at + width))
    at = at + width
    branch[...] = total
    middle = mixed[...] + total * rms_factor(total) * gains[1:2, :]
    grad_middle[...] = middle
    tokens = (middle * rms_factor(middle) * gains[2:3, :]).astype(BF)
    keep[:, first] = tokens
    give[:, first] = tokens
    leave(None, first)

    def put(k, j, value):
        out = keep if k < 2 else give
        cols = slice(((k % 2) * 3 + j) * padded, ((k % 2) * 3 + j + 1) * padded)
        out[:, cols] = value
        leave(k // 2, cols)

    result = jnp.zeros_like(total)
    for k in range(TP):

        @pl.when(own_slot == k)
        def _():
            for copy in own(k):
                copy.wait()

        @pl.when(own_slot != k)
        def _():
            others(k).wait()

        gate = dot_t(keep[:, first], weights[k, 0])
        up = dot_t(keep[:, first], weights[k, 1])
        gates[k] = gate
        ups[k] = up
        act = (gate * jax.nn.sigmoid(gate) * up).astype(BF)
        put(k, 2, act)
        result = result + dot(act, weights[k, 2])
    middle = grad_middle[...]
    latents[...] = (middle + result * rms_factor(result) * gains[3:4, :]).astype(BF)

    grad_block = cot[...].astype(F32) * active
    grad_result, sums[2:3, :] = back(result, gains[3:4, :], grad_block)
    grad_result = grad_result.astype(BF)
    keep[:, second] = grad_result
    give[:, second] = grad_result
    leave(None, second)
    grad_hidden_in = jnp.zeros_like(total)
    for k in range(TP):
        grad_hidden = dot_t(keep[:, second], weights[k, 2])
        gate, up = gates[k], ups[k]
        squashed = jax.nn.sigmoid(gate)
        grad_gate = (grad_hidden * up * squashed * (1.0 + gate * (1.0 - squashed))).astype(BF)
        grad_up = (grad_hidden * gate * squashed).astype(BF)
        put(k, 0, grad_gate)
        put(k, 1, grad_up)
        grad_hidden_in = grad_hidden_in + dot(grad_gate, weights[k, 0])
        grad_hidden_in = grad_hidden_in + dot(grad_up, weights[k, 1])
    grad, sums[1:2, :] = back(grad_middle[...], gains[2:3, :], grad_hidden_in)
    grad = cot[...].astype(F32) * active + grad
    grad_middle[...] = grad
    grad, sums[0:1, :] = back(branch[...], gains[1:2, :], grad)
    grad = grad.astype(BF)

    @pl.when(core == 0)
    def _():
        keep[:, at:] = grad[:, :half]
        give[:, at:] = grad[:, half:]

    @pl.when(core != 0)
    def _():
        keep[:, at:] = grad[:, half:]
        give[:, at:] = grad[:, :half]

    leave(None, slice(at, at + half))
    g0[...] = dot_t(grad, output_own[...]).astype(BF)
    for k, out in ((1, g1), (2, g2), (3, g3)):
        out[...] = dot_t(grad, output_rest[k - 1]).astype(BF)
    sums[3:, :] = jnp.zeros((sums.shape[0] - 3, sums.shape[1]), F32)
    for _, copy in leaving:
        copy.wait()


def back(value, gain, grad):
    factor = rms_factor(value)
    scaled = grad * gain
    grad_value = factor * scaled - value * (factor * factor * factor) * jnp.mean(
        value * scaled, axis=-1, keepdims=True
    )
    return grad_value, jnp.sum(grad * value * factor, axis=0, keepdims=True)


def middle_part(
    meta, mixed, ctx, output_own, output_mine, output_theirs, gains, cot, gate_up, down, ffn
):
    rows, width = mixed.shape
    wide = ctx[0].shape[1]
    padded = ffn.shape[2]
    vmem = pl.BlockSpec(memory_space=pltpu.VMEM)
    anywhere = pl.BlockSpec(memory_space=pl.ANY)
    shape = (rows, 6 * padded + 3 * width + width // 2)
    acts = pltpu.HBM(shape, BF)
    hbm = pl.BlockSpec(memory_space=pltpu.HBM)
    return pl.pallas_call(
        middle_kernel,
        out_shape=(
            pltpu.HBM((rows, width), BF),
            pltpu.HBM((rows, width), F32),
        )
        + (jax.ShapeDtypeStruct((rows, wide), BF),) * TP
        + (acts, acts, jax.ShapeDtypeStruct((8, width), F32)),
        in_specs=[pl.BlockSpec(memory_space=pltpu.SMEM)] + [vmem] * 10 + [anywhere] * 3,
        out_specs=(vmem,) * (2 + TP) + (hbm, hbm, vmem),
        scratch_shapes=[
            pltpu.VMEM((TP, 3, padded, width), BF),
            pltpu.VMEM((TP, rows, padded), F32),
            pltpu.VMEM((TP, rows, padded), F32),
            pltpu.VMEM((rows, width), F32),
            pltpu.VMEM((TP - 1, wide, width), BF),
            pltpu.VMEM(shape, BF),
            pltpu.VMEM(shape, BF),
            pltpu.SemaphoreType.DMA((TP + 1,)),
            pltpu.SemaphoreType.DMA((2, 10)),
        ],
        compiler_params=pltpu.CompilerParams(vmem_limit_bytes=56 * 2**20),
        name="middle",
    )(
        meta, mixed, *ctx, output_own, output_mine, output_theirs, gains, cot, gate_up, down, ffn
    )


def gradients_kernel(
    mine, theirs, first, first_other, second, second_other, c0, c0_other, c1, c1_other, b, b_other, out, *output
):
    half = first.shape[1]

    def both(left, right):
        return jnp.concatenate([left[...], right[...]], axis=0)

    @pl.when(pl.program_id(0) == 0)
    def _():
        for i, (ctx, other) in enumerate(((c0, c0_other), (c1, c1_other))):
            total = t_dot(both(ctx, other), both(b, b_other))
            for j in range(2):
                output[2 * i + j][...] = total[j * half // 2 : (j + 1) * half // 2].astype(BF)

    tokens = jnp.concatenate([both(first, first_other), both(second, second_other)], axis=1)
    total = t_dot(both(mine, theirs), tokens)
    rows, cols = out.shape[2], out.shape[3]
    for i in range(4):
        for j in range(4):
            piece = total[i * rows : (i + 1) * rows, j * cols : (j + 1) * cols]
            out[4 * i + j, 0] = piece.astype(BF)


def gradients(mine, theirs, hidden, padded, width):
    rows = mine.shape[0]
    half = width // 2
    first = 6 * padded // half
    acts = pl.BlockSpec((rows, padded), lambda i: (0, i))

    def token(side):
        return pl.BlockSpec((rows, half), lambda i: (0, first + 2 * (lax.rem(i, 3) // 2) + side))

    shape = (CHIPS, 6, hidden // 4, width // 4)
    return pl.pallas_call(
        gradients_kernel,
        grid=(6,),
        in_specs=[acts, acts, token(0), token(0), token(1), token(1)]
        + [pl.BlockSpec((rows, half), lambda i, at=at: (0, first + at)) for at in (4, 4, 5, 5, 6, 6)],
        out_specs=(pl.BlockSpec((CHIPS, 1) + shape[2:], lambda i: (0, i, 0, 0)),)
        + (pl.BlockSpec((width // TP, half), lambda i: (0, 0)),) * TP,
        out_shape=(pltpu.HBM(shape, BF),) + (pltpu.HBM((width // TP, half), BF),) * TP,
        compiler_params=pltpu.CompilerParams(vmem_limit_bytes=22 * 2**20),
        name="gradients",
    )(*[*in_hbm(mine), theirs] * 6)


def widen_kernel(meta, mine, theirs, gate_up, down):
    core = meta[0]
    units, part = mine.shape[2], mine.shape[3]
    for owner, shares in ((core, mine), (1 - core, theirs)):
        for i in range(4):
            for j in range(4):
                rows = slice(i * units, (i + 1) * units)
                cols = pl.ds(pl.multiple_of((2 * j + owner) * part, part), part)
                gate_up[:, rows, cols] = shares[4 * i + j, :2].astype(F32)
                down[rows, cols] = shares[4 * i + j, 2].astype(F32)


def widen(meta, mine, theirs, hidden):
    width = 8 * mine.shape[3]
    vmem = pl.BlockSpec(memory_space=pltpu.VMEM)
    return pl.pallas_call(
        widen_kernel,
        out_shape=(
            jax.ShapeDtypeStruct((2, hidden, width), F32),
            jax.ShapeDtypeStruct((hidden, width), F32),
        ),
        in_specs=[pl.BlockSpec(memory_space=pltpu.SMEM)] + [vmem] * 2,
        out_specs=(vmem, vmem),
        compiler_params=pltpu.CompilerParams(vmem_limit_bytes=20 * 2**20),
        name="widen",
    )(meta, mine, theirs)


def proj_grads_kernel(meta, p0, p1, p2, p3, p4, p5, p6, p7, grads, keep, give, normed, total):
    tp, core = meta[0], meta[2]
    part = p0.shape[0]
    for k, piece in enumerate((p0, p1, p2, p3, p4, p5, p6, p7)):
        place = lax.rem(tp + (TP - k // 2), TP) * (2 * part) + (k % 2) * part
        normed[pl.ds(pl.multiple_of(place, part), part), :] = piece[...]
    total[...] = t_dot(normed[...], grads[...])
    half = keep.shape[0]
    keep[...] = total[pl.ds(pl.multiple_of(core * half, half), half), :].astype(BF)
    give[...] = total[pl.ds(pl.multiple_of((1 - core) * half, half), half), :].astype(BF)


def proj_gradients(meta, pieces, grads):
    length, columns = grads.shape
    width = pieces[0].shape[1]
    vmem = pl.BlockSpec(memory_space=pltpu.VMEM)
    return pl.pallas_call(
        proj_grads_kernel,
        out_shape=(jax.ShapeDtypeStruct((width // 2, columns), BF),) * 2,
        in_specs=[pl.BlockSpec(memory_space=pltpu.SMEM)] + [vmem] * 9,
        out_specs=(vmem,) * 2,
        scratch_shapes=[pltpu.VMEM((length, width), BF), pltpu.VMEM((width, columns), F32)],
        compiler_params=pltpu.CompilerParams(vmem_limit_bytes=20 * 2**20),
        name="proj_gradients",
    )(meta, *pieces, grads)


def pack_kernel(mine, theirs, o0, o1, o2, o3, out):
    chips, _, wide = out.shape
    lines = mine.shape[0] // chips
    bands = o0.shape[0] // chips
    total = o0[...].astype(F32) + o1[...].astype(F32) + o2[...].astype(F32) + o3[...].astype(F32)
    total = total.astype(BF)
    for i in range(chips):
        for h in range(2):
            where = (slice(i * bands, (i + 1) * bands), slice(h * wide, (h + 1) * wide))
            out[i, h * bands : (h + 1) * bands, :] = total[where]
        at = 2 * bands
        for m in range(3):
            where = (slice(i * lines, (i + 1) * lines), slice(m * wide, (m + 1) * wide))
            part = mine[where].astype(F32) + theirs[where].astype(F32)
            out[i, at + m * lines : at + (m + 1) * lines, :] = part.astype(BF)


def pack(mine, theirs, output_parts):
    rows, columns = mine.shape
    wide = columns // 3
    vmem = pl.BlockSpec(memory_space=pltpu.VMEM)
    return pl.pallas_call(
        pack_kernel,
        out_shape=jax.ShapeDtypeStruct((CHIPS, (3 * rows + 2 * wide) // CHIPS, wide), BF),
        in_specs=[vmem] * 6,
        out_specs=vmem,
        compiler_params=pltpu.CompilerParams(vmem_limit_bytes=10 * 2**20),
        name="pack",
    )(mine, theirs, *in_hbm(*output_parts))


def unpack_kernel(meta, mine, theirs, output, proj, adapter):
    core = meta[0]
    chips, _, wide = mine.shape
    bands = wide // chips
    lines = proj.shape[1] // 2 // chips
    rows = adapter.shape[0] // 2 // chips
    for owner, part in ((core, mine), (1 - core, theirs)):
        for i in range(chips):
            for j in range(2):
                cols = pl.ds(pl.multiple_of((2 * owner + j) * wide, wide), wide)
                output[i * bands : (i + 1) * bands, cols] = part[
                    i, j * bands : (j + 1) * bands
                ].astype(F32)
            at = 2 * bands
            place = pl.ds(pl.multiple_of((owner * chips + i) * lines, lines), lines)
            for m in range(3):
                proj[m, place, :] = part[i, at + m * lines : at + (m + 1) * lines].astype(F32)
            at = at + 3 * lines
            place = pl.ds(pl.multiple_of((owner * chips + i) * rows, rows), rows)
            adapter[place, :] = part[i, at:].astype(F32)


def unpack(meta, mine, theirs, width):
    wide = mine.shape[2]
    vmem = pl.BlockSpec(memory_space=pltpu.VMEM)
    return pl.pallas_call(
        unpack_kernel,
        out_shape=(
            jax.ShapeDtypeStruct((wide, width), F32),
            jax.ShapeDtypeStruct((3, width, wide), F32),
            jax.ShapeDtypeStruct((2 * width, wide), F32),
        ),
        in_specs=[pl.BlockSpec(memory_space=pltpu.SMEM)] + [vmem] * 2,
        out_specs=(vmem,) * 3,
        compiler_params=pltpu.CompilerParams(vmem_limit_bytes=16 * 2**20),
        name="unpack",
    )(meta, mine, theirs)


def last_kernel(meta, mine, theirs, flat, adapter, sums, latents, parts, home):
    tp = meta[0]
    rows, width = mine.shape
    wide = parts.shape[2]
    for k in range(TP):
        where = pl.ds(pl.multiple_of(lax.rem(tp + (TP - k), TP) * wide, wide), wide)
        total = t_dot(flat[0], mine[:, where]) + t_dot(flat[1], theirs[:, where])
        parts[k, :width, :] = total.astype(BF)
        parts[k, width:, :] = jnp.concatenate(
            [sums[:, where], jnp.zeros((24, wide), F32)], axis=0
        ).astype(BF)
    for j, grad in enumerate((mine, theirs)):
        back_to = dot_t(grad[...], adapter[...]).reshape(GRP, rows // GRP, width)
        home[:, j] = back_to.astype(BF)
    home[:, 2] = latents[...].astype(F32).reshape(GRP, rows // GRP, width).astype(BF)


def last(meta, mine, theirs, flat, adapter, sums, latents):
    rows, width = mine.shape
    vmem = pl.BlockSpec(memory_space=pltpu.VMEM)
    return pl.pallas_call(
        last_kernel,
        out_shape=(
            jax.ShapeDtypeStruct((TP, width + 32, width // TP), BF),
            pltpu.HBM((GRP, 3, rows // GRP, width), BF),
        ),
        in_specs=[pl.BlockSpec(memory_space=pltpu.SMEM)] + [vmem] * 6,
        out_specs=(vmem, vmem),
        compiler_params=pltpu.CompilerParams(vmem_limit_bytes=16 * 2**20),
        name="last",
    )(meta, mine, theirs, flat, adapter, sums, latents)


def body(
    embedded,
    start_state,
    cotangent,
    lengths,
    group_depth,
    assignment,
    adapter_weight,
    norm_gains,
    projections,
    output_weight,
    gate_up_weight,
    down_weight,
):
    group = lax.axis_index("grp").astype(jnp.int32)
    tp = lax.axis_index("tp").astype(jnp.int32)
    core, x, y = lax.rem(group, 2), lax.div(group, 8), lax.rem(lax.div(group, 2), 4)
    rows, width = embedded.shape[2] * GRP, embedded.shape[3]
    wide = projections.shape[2]
    hidden = down_weight.shape[0]
    share = -(-hidden // (8 * GRP)) * 8

    def pick(first, second):
        return jnp.where(core == 0, first, second)

    gate_up = gate_up_weight.transpose(0, 2, 1)
    pad = ((0, 0), (0, share * GRP - hidden), (0, 0))
    ffn = jnp.concatenate(
        [
            lax.dynamic_slice_in_dim(jnp.pad(gate_up, pad), group * share, share, axis=1),
            lax.dynamic_slice_in_dim(jnp.pad(down_weight[None], pad), group * share, share, axis=1),
        ]
    )

    outgoing = route(assignment, start_state[:, 0], embedded[:, 0], cotangent[:, 0])
    joined = lax.all_to_all(outgoing, "grp", split_axis=0, concat_axis=0, tiled=True)

    position = jnp.argmax(assignment == group)
    length = lengths[position]
    active = (group_depth[group] > 0).astype(jnp.int32)
    meta = jnp.stack([tp, length, core, active])

    half = lax.dynamic_slice_in_dim(adapter_weight, core * width, width, axis=0)
    half = jnp.concatenate([half, jnp.pad(norm_gains, ((0, 28), (0, 0)))], axis=0)
    half_pieces = gather_halves(half)
    adapter, gains = assemble(meta, half_pieces)
    ffn_pieces = gather_pieces(after(ffn, *half_pieces[2:4], *half_pieces[6:]))[1:]
    ffn = jnp.concatenate([after(piece, joined) for piece in ffn_pieces])
    ffn = lax.all_gather(ffn, "grp", axis=1, tiled=True).reshape(TP - 1, 3, share * GRP, width)

    cosine, sine = [jnp.asarray(v) for v in rope_tables(rows * TP)]

    mixed, theirs, flat, grad_state = adapt(joined, adapter)
    mixed = mixed + to_partner(theirs).astype(F32)
    normed = (mixed * rms_factor(mixed) * gains[0]).astype(BF)
    normed_halves = gather_halves(normed)
    output_half = lax.dynamic_slice_in_dim(
        output_weight, core * (width // 2), width // 2, axis=1
    )
    output_half = after(output_half, *normed_halves[2:])
    output_mine = [send(output_half, -k) for k in range(1, TP)]
    ctx, qkv, probs = attend(
        meta, normed_halves, projections, cosine, sine
    )
    ctx_pieces = [ctx[0]] + [send(ctx[k], -k) for k in range(1, TP)]
    output_mine = jnp.stack([after(v, ctx) for v in output_mine])
    latents, grad_middle, g0, g1, g2, g3, mine, give, sums = middle_part(
        meta, mixed, ctx_pieces, output_weight, output_mine, to_partner(output_mine), gains, grad_state,
        gate_up, down_weight, ffn,
    )

    theirs = to_partner(give)
    g1, g2, g3 = [send(g, k) for k, g in ((1, g1), (2, g2), (3, g3))]
    theirs, g1, g2, g3 = lax.optimization_barrier((theirs, g1, g2, g3))

    cuts, *output_parts = gradients(mine, theirs, hidden, share * GRP, width)
    ffn_sum = lax.psum_scatter(
        cuts.reshape(-1, width // 4), "grp", scatter_dimension=0, tiled=True, axis_index_groups=SAME_CORE
    ).reshape(6, -1, width // 4)

    grad_qkv, *normed_parts = attend_back(
        after(meta, cuts), [g0, g1, g2, g3], cosine, sine, qkv, probs, projections
    )
    output_parts = output_parts[:1] + [send(output_parts[k], k) for k in range(1, TP)]
    grad_normed = scatter_halves([after(v, *output_parts[1:]) for v in normed_parts])
    keep, give = proj_gradients(meta, normed_halves, grad_qkv)
    some_part = pack(keep, to_partner(give), output_parts)
    grad_normed = after(grad_normed, some_part)

    grad_mixed, gain_one = rms_back(mixed, gains[0], grad_normed)
    grad_mixed = (grad_middle + grad_mixed).astype(BF)
    sums = jnp.concatenate([gain_one[None], sums[:7]])
    parts, home = last(meta, grad_mixed, to_partner(grad_mixed), flat, adapter, sums, latents)

    adapter_sum = scatter_halves([parts[k] for k in range(TP)]).astype(BF)
    ffn_sum = after(ffn_sum, adapter_sum)
    total = send_by_core(ffn_sum[:3], 0, 2).astype(F32)
    total = total + send_by_core(ffn_sum[3:], -1, -3).astype(F32)
    total = total + to_partner(total.astype(BF)).astype(F32)
    total = lax.dynamic_slice_in_dim(total, core * (width // 8), width // 8, axis=2).astype(BF)
    ffn_part = total

    total = adapter_sum
    lines = width // CHIPS
    gains_part = jnp.broadcast_to(total[None, width : width + 8], (CHIPS, 8, wide))
    total = jnp.concatenate(
        [some_part, total[:width].reshape(CHIPS, lines, wide), gains_part], axis=1
    )
    total = reduce_chips(total)
    at = total.shape[0] - 8
    grad_gains = total[at : at + 4]
    grad_gains = grad_gains + to_partner(grad_gains)
    small = total[:at].astype(BF)
    ffn_sum = gather_chips(after(ffn_part, small))
    small = lax.all_gather(small, "grp", axis=0, tiled=False, axis_index_groups=SAME_CORE)

    home = after(home, ffn_sum)
    home = lax.all_to_all(home, "grp", split_axis=0, concat_axis=0, tiled=True)

    here = jnp.stack([core, x, y])
    grad_gate_up, grad_down = widen(here, ffn_sum, to_partner(ffn_sum), hidden)

    home = after(home, grad_down)
    latents, grad_embedded, grad_start = finish(
        assignment, group_depth, home, start_state[:, 0], cotangent[:, 0]
    )

    small = after(small, latents)
    grad_output, grad_proj, grad_adapter = unpack(here, small, to_partner(small), width)

    return (
        latents[:, None],
        grad_embedded[:, None],
        grad_start[:, None],
        grad_adapter,
        grad_gains,
        grad_proj,
        grad_output,
        grad_gate_up.transpose(0, 2, 1),
        grad_down,
    )


def solution(mesh):
    tokens = P(None, "tp", "grp", None)
    weights = (
        P(None, "tp"),
        P(None, "tp"),
        P(None, None, "tp"),
        P("tp", None),
        P(None, None, "tp"),
        P("tp", None),
    )
    return jax.shard_map(
        body,
        mesh=mesh,
        in_specs=(tokens, tokens, tokens, P(), P(), P()) + weights,
        out_specs=(tokens, tokens, tokens) + weights,
        check_vma=False,
    )
```
